128 devices in a mesh: dp: 32 (over x, z, core), cent: 4 (over y).
Axes of the slice: x: 4, y: 4, z: 4, core: 2. Of those that a mesh axis runs over, the one named last changes fastest.
Arguments:
- embeddings: bfloat16 [32768, 512], P('dp'), may hold values from -60 to 60, as said below
- centroids: bfloat16 [16384, 512], P('cent'), may hold values from -60 to 60, as said below
Outputs:
- new_centroids: float32 [16384, 512], P(('cent', 'dp'))
- column_mass: float32 [16384], P(('cent', 'dp'))
The draws below stay inside these ranges and needn't reach their ends.
Inputs may be any that keep to these rules, and one draw needn't show every extreme that they name: `embeddings`: every row is nonzero. `centroids`: every row is nonzero.
All inputs are finite; a program needn't handle non-finite values.
Results may differ from the reference program's by a relative error of at most 0.00074.
Values sent between devices are 32-bit elements; how exact they have to be, the bound alone decides.
No kernel may reach another device: no remote copies, remote signals or barrier semaphores. Data moves between devices by JAX's collectives and lax.ppermute only.
A program may use at most 128 MiB of HBM per device.

```python
import math
import jax
import jax.numpy as jnp
from jax import lax

D = 512
K = 16384
ROWS_DEV = 1024
ITERS = 3
ROWS = 32768
N_DP = 32


def cluster_directions(key, width):
    common = jax.random.fold_in(key, 5)
    return jnp.clip(jax.random.normal(common, (8, width), jnp.float32), -4.0, 4.0)


def cluster_members(key, salt, count):
    first, second = jax.random.split(jax.random.fold_in(key, salt))
    cluster_order = jax.random.permutation(first, 8)
    ticket = jax.random.randint(second, (count,), 0, 36)
    bucket_edges = jnp.array([1, 3, 6, 10, 15, 21, 28], jnp.int32)
    bucket = jnp.sum((ticket[:, None] >= bucket_edges[None, :]).astype(jnp.int32), axis=1)
    return jnp.take(cluster_order, bucket, axis=0)


def scaled_rows(key, salt, count, width):
    directions = cluster_directions(key, width)
    members = cluster_members(key, salt + 1, count)
    first, second, third = jax.random.split(jax.random.fold_in(key, salt), 3)
    row_scale = jnp.exp(jax.random.uniform(second, (count, 1), jnp.float32, 0.0, math.log(10.0)))
    strength = jax.random.uniform(third, (count, 1), jnp.float32, 0.5, 1.0)
    noise_part = jnp.clip(jax.random.normal(first, (count, width), jnp.float32), -5.0, 5.0)
    picked = jnp.take(directions, members, axis=0)
    return jnp.clip(noise_part + strength * picked, -6.0, 6.0) * row_scale


def draw_embeddings(key, part):
    return scaled_rows(key, 11, ROWS, D).astype(jnp.bfloat16)


def draw_centroids(key, part):
    return scaled_rows(key, 23, K, D).astype(jnp.bfloat16)


def setup_inputs(seed: int = 0) -> dict:
    arg_keys = jax.random.split(jax.random.key(seed), 3)
    return {
        "embeddings": draw_embeddings(jax.random.fold_in(arg_keys[2], 71), 0),
        "centroids": draw_centroids(jax.random.fold_in(arg_keys[2], 71), 0),
    }


TAU = 0.02

def rms_rows(values):
    wide = values.astype(jnp.float32)
    return (wide * lax.rsqrt(lax.optimization_barrier(jnp.mean(wide * wide, axis=1, keepdims=True)) + 1e-06)).astype(jnp.bfloat16)

def energy_block(rows_block, cent_rows):
    scores = lax.dot_general(rows_block, cent_rows, (((1,), (1,)), ((), ())), preferred_element_type=jnp.float32)
    return jnp.exp(scores * (1.0 / (TAU * D)))

def reference(embeddings, centroids):
    high = lax.Precision.HIGHEST
    xh = rms_rows(embeddings)
    ch = rms_rows(centroids)
    blocks = xh.reshape(N_DP, ROWS_DEV, D)
    ratio = float(ROWS) / float(K)

    def sums(u, v):

        def step(carry, item):
            block, weights = item
            energy = energy_block(block, ch)
            rows_sum = jnp.dot(energy, v, precision=high)
            return (carry + jnp.dot(weights, energy, precision=high), rows_sum)
        cols, rows_sum = lax.scan(step, jnp.zeros((K,), jnp.float32), (blocks, u.reshape(N_DP, ROWS_DEV)))
        return (rows_sum.reshape(ROWS), cols)
    u = jnp.ones((ROWS,), jnp.float32)
    v = jnp.ones((K,), jnp.float32)
    for step_index in range(ITERS):
        rows_sum, cols = sums(u, v)
        u, v = (jnp.sqrt(u / rows_sum), jnp.sqrt(v * ratio / cols))

    def final_step(carry, item):
        cols, weighted = carry
        block, weights = item
        energy = energy_block(block, ch)
        cols = cols + jnp.dot(weights, energy, precision=high)
        plan = (float(K) * weights[:, None] * energy * v[None, :]).astype(jnp.bfloat16)
        weighted = weighted + lax.dot_general(plan, block, (((0,), (0,)), ((), ())), preferred_element_type=jnp.float32)
        return ((cols, weighted), None)
    init = (jnp.zeros((K,), jnp.float32), jnp.zeros((K, D), jnp.float32))
    (cols, weighted), unused = lax.scan(final_step, init, (blocks, u.reshape(N_DP, ROWS_DEV)))
    column_mass = v * cols * (float(K) / float(ROWS))
    new_centroids = weighted * lax.rsqrt(lax.optimization_barrier(jnp.mean(weighted * weighted, axis=1, keepdims=True)) + 1e-06)
    return (new_centroids, column_mass)
```

```python
import functools

import jax
import jax.numpy as jnp
from jax import lax
from jax.experimental import pallas as pl
from jax.experimental.pallas import tpu as pltpu
from jax.sharding import PartitionSpec as P

ITERS = 3
TAU = 0.02
NX, NZ, NC, NY = 4, 4, 2, 4
F32, BF16 = jnp.float32, jnp.bfloat16
VM = pltpu.VMEM
LIMIT = 16 * 1024 * 1024


def index(x, z, c):
    return (x * NZ + z) * NC + c


def shift_dp(value, dx, dz, dc):
    pairs = [
        (index(x, z, c), index((x + dx) % NX, (z + dz) % NZ, (c + dc) % NC))
        for x in range(NX)
        for z in range(NZ)
        for c in range(NC)
    ]
    return lax.ppermute(value, "dp", pairs)


def flip_y(value, bit):
    return lax.ppermute(value, "cent", [(i, i ^ bit) for i in range(NY)])


def vmem(value):
    return pltpu.with_memory_space_constraint(value, VM)


def call(body, outs, *args, smem=0, **kw):
    specs = [pl.BlockSpec(memory_space=pltpu.SMEM)] * smem
    specs += [pl.BlockSpec(memory_space=VM)] * (len(args) - smem)
    args = list(args[:smem]) + [vmem(a) for a in args[smem:]]
    return pl.pallas_call(
        body,
        in_specs=specs,
        out_specs=[pl.BlockSpec(memory_space=VM)] * len(outs),
        out_shape=[VM(shape, dtype) for shape, dtype in outs],
        compiler_params=pltpu.CompilerParams(vmem_limit_bytes=LIMIT),
        **kw,
    )(*args)


def norm_rows(wide):
    mean = jnp.mean(wide * wide, axis=1, keepdims=True)
    return wide * lax.rsqrt(mean + 1e-06)


def normalize(emb_ref, wide_ref, xh_ref):
    def step(i, carry):
        rows = pl.ds(pl.multiple_of(i * 128, 128), 128)
        xh = norm_rows(emb_ref[rows, :].astype(F32)).astype(BF16)
        xh_ref[rows, :] = xh
        wide_ref[rows, :] = xh.astype(F32)
        return carry

    lax.fori_loop(0, emb_ref.shape[0] // 128, step, 0, unroll=2)


def lane_total(acc_ref):
    ones = jnp.ones((8, 128), F32)
    total = lax.dot_general(
        ones,
        acc_ref[...],
        (((1,), (1,)), ((), ())),
        precision=lax.Precision.HIGHEST,
        preferred_element_type=F32,
    )
    return total[0:1, :]


def fold_lanes(block):
    total = block[:, 0:128]
    for t in range(1, block.shape[1] // 128):
        total = total + block[:, t * 128 : (t + 1) * 128]
    return total


def fold_rows(block):
    return jnp.sum(block.reshape(block.shape[0] // 8, 8, block.shape[1]), axis=0)


def scores_exp(ch, xh):
    width = xh.shape[1]
    scores = lax.dot_general(ch, xh, (((1,), (1,)), ((), ())), preferred_element_type=F32)
    return jnp.exp(scores * (1.0 / (TAU * width)))


BLK = 256


def energy_own(core_ref, cents_ref, xh_ref, et_ref, ch_ref, acc_ref, r_ref):
    core = core_ref[0]
    n_blocks = ch_ref.shape[0] // BLK
    parts = BLK // 128

    def step(i, r_acc):
        rows = pl.ds(pl.multiple_of(i * BLK, BLK), BLK)
        for k in range(parts):
            part = cents_ref[i * parts + k, core].astype(F32)
            ch_ref[pl.ds(pl.multiple_of(i * BLK + k * 128, 128), 128), :] = norm_rows(part).astype(
                BF16
            )
        e = scores_exp(ch_ref[rows, :], xh_ref[...])
        et_ref[rows, :] = e
        acc_ref[rows, :] = fold_lanes(e)
        return r_acc + fold_rows(e)

    r_acc = lax.fori_loop(0, n_blocks, step, jnp.zeros((8, xh_ref.shape[0]), F32), unroll=2)
    r_ref[...] = jnp.sum(r_acc, axis=0, keepdims=True)


def energy_peer(ch_ref, wide_ref, acc_ref, r_own_ref, et_ref, xh_ref, r_ref, c_ref, tot_ref):
    n_blocks = ch_ref.shape[0] // BLK
    xh_ref[...] = wide_ref[...].astype(BF16)

    def step(i, r_acc):
        rows = pl.ds(pl.multiple_of(i * BLK, BLK), BLK)
        e = scores_exp(ch_ref[rows, :], xh_ref[...])
        et_ref[rows, :] = e
        tot_ref[rows, :] = acc_ref[rows, :] + fold_lanes(e)
        return r_acc + fold_rows(e)

    half = xh_ref.shape[0]
    r_acc = lax.fori_loop(0, n_blocks, step, jnp.zeros((8, half), F32), unroll=2)
    r_ref[:, 0:half] = r_own_ref[...]
    r_ref[:, half:] = jnp.sum(r_acc, axis=0, keepdims=True)
    c_ref[...] = lane_total(tot_ref)


def new_uv(ratio, u_ref, v_ref, r_refs, c_refs):
    r = r_refs[0][...] + r_refs[1][...]
    c = (c_refs[0][...] + c_refs[1][...]) + (c_refs[2][...] + c_refs[3][...])
    return jnp.sqrt(u_ref[...] / r), jnp.sqrt(v_ref[...] * ratio / c)


def spread_column(row, out_ref):
    for t in range(row.shape[1] // 128):
        block = jnp.broadcast_to(row[:, t * 128 : (t + 1) * 128], (128, 128))
        out_ref[t * 128 : (t + 1) * 128, :] = block.T


def scale_pass(ratio, *refs):
    (eta_ref, etb_ref, u_ref, v_ref, r0, r1, c0, c1, c2, c3) = refs[:10]
    (uo_ref, vo_ref, ro_ref, co_ref, vcol_ref, acc_ref) = refs[10:]
    u, v = new_uv(ratio, u_ref, v_ref, (r0, r1), (c0, c1, c2, c3))
    uo_ref[...] = u
    vo_ref[...] = v
    spread_column(v, vcol_ref)
    half = eta_ref.shape[1]
    tiles = half // 128
    ub = [jnp.broadcast_to(u[:, t * 128 : (t + 1) * 128], (8, 128)) for t in range(2 * tiles)]

    def step(i, carry):
        rows = pl.ds(pl.multiple_of(i * 8, 8), 8)
        vb = vcol_ref[rows, :]
        out, parts = [], []
        for t in range(2 * tiles):
            ref = eta_ref if t < tiles else etb_ref
            e = ref[rows, (t % tiles) * 128 : (t % tiles + 1) * 128]
            out.append(carry[t] + e * vb)
            parts.append(e * ub[t])
        while len(parts) > 1:
            parts = [a + b for a, b in zip(parts[::2], parts[1::2])]
        acc_ref[rows, :] = parts[0]
        return tuple(out)

    zero = jnp.zeros((8, 128), F32)
    acc = lax.fori_loop(0, eta_ref.shape[0] // 8, step, (zero,) * (2 * tiles), unroll=4)
    for t in range(2 * tiles):
        ro_ref[:, t * 128 : (t + 1) * 128] = jnp.sum(acc[t], axis=0, keepdims=True)
    co_ref[...] = lane_total(acc_ref)


def plan_first(ratio, big, pos_ref, *refs):
    (eta_ref, etb_ref, xa_ref, xb_ref, u_ref, v_ref, r0, r1, c0, c1, c2, c3) = refs[:12]
    (ku_ref, vo_ref, vcol_ref, a2_ref, b2_ref) = refs[12:]
    u, v = new_uv(ratio, u_ref, v_ref, (r0, r1), (c0, c1, c2, c3))
    ku_ref[...] = big * u
    vo_ref[...] = v
    spread_column(v, vcol_ref)
    etx = (eta_ref, etb_ref, xa_ref, xb_ref, ku_ref, vcol_ref)
    piece_a(pos_ref, 2, a2_ref, *etx)
    piece_b(pos_ref, 2, b2_ref, *etx)


def weigh(starts, out_ref, offset, eta_ref, etb_ref, xa_ref, xb_ref, ku_ref, vcol_ref):
    half = eta_ref.shape[1]
    sums, qa, qb = [], [], []
    for s in starts:
        rows = pl.ds(pl.multiple_of(s, 64), 64)
        vb = vcol_ref[rows, :]
        total = jnp.zeros((64, 128), F32)
        for ref, base, qs in ((eta_ref, 0, qa), (etb_ref, half, qb)):
            tiles = []
            for t in range(half // 128):
                lanes = slice(t * 128, (t + 1) * 128)
                scaled = ku_ref[:, base + t * 128 : base + (t + 1) * 128] * ref[rows, lanes]
                total = total + scaled
                tiles.append((scaled * vb).astype(BF16))
            qs.append(jnp.concatenate(tiles, axis=1))
        sums.append(total)
    out_ref[offset : offset + 64 * len(starts), :] = jnp.dot(
        jnp.concatenate(qa, axis=0), xa_ref[...], preferred_element_type=F32
    ) + jnp.dot(jnp.concatenate(qb, axis=0), xb_ref[...], preferred_element_type=F32)
    return sums


def piece_a(pos_ref, d, out_ref, *etx):
    base = lax.rem(pos_ref[0] + d, NX) * (NZ * 128)
    eta_ref, etb_ref, _, _, ku_ref, _ = etx
    half = eta_ref.shape[1]
    low = weigh([base + k * 128 for k in range(NZ)], out_ref, 0, *etx)
    ones = jnp.ones((8, 128), F32)
    rows8 = out_ref.shape[0] - 8
    for k in range(NZ):
        rows = pl.ds(pl.multiple_of(base + k * 128 + 64, 64), 64)
        total = jnp.zeros((64, 128), F32)
        for ref, off in ((eta_ref, 0), (etb_ref, half)):
            for t in range(half // 128):
                total = total + (
                    ku_ref[:, off + t * 128 : off + (t + 1) * 128]
                    * ref[rows, t * 128 : (t + 1) * 128]
                )
        both = jnp.concatenate([low[k], total], axis=0)
        out_ref[rows8:, k * 128 : (k + 1) * 128] = lax.dot_general(
            ones,
            both,
            (((1,), (1,)), ((), ())),
            precision=lax.Precision.HIGHEST,
            preferred_element_type=F32,
        )


def piece_b(pos_ref, d, out_ref, *etx):
    base = lax.rem(pos_ref[1] + d, NZ) * 128 + 64
    weigh([base + k * (NZ * 128) for k in range(NX)], out_ref, 0, *etx)


def plan_rest(pos_ref, *refs):
    etx = refs[:6]
    outs = refs[6:]
    for n, d in enumerate((1, 3, 0)):
        piece_a(pos_ref, d, outs[2 * n], *etx)
        piece_b(pos_ref, d, outs[2 * n + 1], *etx)


HALF_A = 128
HALF_B = 128


def add_transit(a1, a3, b1, b3, ar, al, br, bl, oa1, oa3, ob1, ob3):
    oa1[0:HALF_A, :] = a1[0:HALF_A, :] + ar[...]
    oa1[HALF_A:, :] = a1[HALF_A:, :]
    oa3[0:HALF_A, :] = a3[0:HALF_A, :]
    oa3[HALF_A:, :] = a3[HALF_A:, :] + al[...]
    ob1[0:HALF_B, :] = b1[0:HALF_B, :] + br[...]
    ob1[HALF_B:, :] = b1[HALF_B:, :]
    ob3[0:HALF_B, :] = b3[0:HALF_B, :]
    ob3[HALF_B:, :] = b3[HALF_B:, :] + bl[...]


def second_pieces(pos_ref, a0, ar, al, b0, br, bl, *outs):
    last = a0.shape[0] - 8
    for d in range(4):
        k = lax.rem(pos_ref[1] + d, NZ)
        rows = pl.ds(pl.multiple_of(k * 64, 64), 64)
        lanes = pl.ds(pl.multiple_of(k * 128, 128), 128)
        outs[d][0:64, :] = a0[rows, :] + ar[rows, :] + al[rows, :]
        outs[d][64:72, 0:128] = a0[last:, lanes] + ar[last:, lanes] + al[last:, lanes]
        outs[d][64:72, 128:] = jnp.zeros((8, 384), F32)
        k = lax.rem(pos_ref[0] + d, NX)
        rows = pl.ds(pl.multiple_of(k * 64, 64), 64)
        outs[4 + d][...] = b0[rows, :] + br[rows, :] + bl[rows, :]


def finish(scale, pos_ref, v_ref, a0, a1, a2, a3, b0, b1, b2, b3, new_ref, mass_ref):
    a = (a0[...] + a1[...]) + (a2[...] + a3[...])
    b = (b0[...] + b1[...]) + (b2[...] + b3[...])
    new_ref[0:64, :] = norm_rows(a[0:64, :])
    new_ref[64:, :] = norm_rows(b)
    start = (pos_ref[0] * NZ + pos_ref[1]) * 128
    v = v_ref[:, pl.ds(pl.multiple_of(start, 128), 128)]
    mass_ref[...] = v * (a[64:65, 0:128] * scale)


def local(embeddings, centroids):
    dp = lax.axis_index("dp")
    core = lax.rem(dp, NC)
    z = lax.rem(dp // NC, NZ)
    x = dp // (NC * NZ)
    core_at = jnp.reshape(core, (1,)).astype(jnp.int32)
    pos = jnp.stack([x, z]).astype(jnp.int32)
    rows, width = embeddings.shape
    all_cents = centroids.shape[0]
    n = all_cents // NC
    total_rows = float(rows * lax.axis_size("dp"))
    total_cents = float(all_cents * lax.axis_size("cent"))
    ratio = total_rows / total_cents

    wide, xa = call(normalize, [((rows, width), F32), ((rows, width), BF16)], embeddings)
    wide_peer = shift_dp(wide, 0, 0, 1)
    cents = centroids.reshape(n // 128, NC, 128, width)
    eta, ch, acc, r_own = call(
        energy_own,
        [((n, rows), F32), ((n, width), BF16), ((n, 128), F32), ((1, rows), F32)],
        core_at,
        cents,
        xa,
        smem=1,
    )
    etb, xb, r, c = call(
        energy_peer,
        [((n, rows), F32), ((rows, width), BF16), ((1, 2 * rows), F32), ((1, n), F32)],
        ch,
        wide_peer,
        acc,
        r_own,
        scratch_shapes=[VM((n, 128), F32)],
    )
    u = jnp.ones((1, 2 * rows), F32)
    v = jnp.ones((1, n), F32)

    def exchange(r, c):
        rc = shift_dp(r, 0, 0, 1)
        cx = [shift_dp(c, d, 0, 0) for d in (1, 2, 3)]
        r = r + jnp.concatenate([rc[:, rows:], rc[:, :rows]], axis=1)
        ry = flip_y(r, 1)
        c = (c + cx[0]) + (cx[1] + cx[2])
        r = r + ry
        cz = [shift_dp(c, 0, d, 0) for d in (1, 2, 3)]
        ry = flip_y(r, 2)
        return (r, ry, c, *cz)

    for step in range(ITERS - 1):
        got = exchange(r, c)
        u, v, r, c = call(
            functools.partial(scale_pass, ratio),
            [((1, 2 * rows), F32), ((1, n), F32), ((1, 2 * rows), F32), ((1, n), F32)],
            eta,
            etb,
            u,
            v,
            *got,
            scratch_shapes=[VM((n, 128), F32)] * 2,
        )
    got = exchange(r, c)
    pa = ((256 + 8, width), F32)
    pb = ((256, width), F32)
    ku, v, vcol, a2, b2 = call(
        functools.partial(plan_first, ratio, total_cents),
        [((1, 2 * rows), F32), ((1, n), F32), ((n, 128), F32), pa, pb],
        pos,
        eta,
        etb,
        xa,
        xb,
        u,
        v,
        *got,
        smem=1,
    )
    ar = shift_dp(a2[:HALF_A], 1, 0, 0)
    br = shift_dp(b2[:HALF_B], 0, 1, 0)
    al = shift_dp(a2[HALF_A:], 3, 0, 0)
    bl = shift_dp(b2[HALF_B:], 0, 3, 0)
    a1, b1, a3, b3, a0, b0 = call(
        plan_rest, [pa, pb] * 3, pos, eta, etb, xa, xb, ku, vcol, smem=1
    )
    a1, a3, b1, b3 = call(add_transit, [pa, pa, pb, pb], a1, a3, b1, b3, ar, al, br, bl)
    ar = shift_dp(a1, 1, 0, 0)
    br = shift_dp(b1, 0, 1, 0)
    al = shift_dp(a3, 3, 0, 0)
    bl = shift_dp(b3, 0, 3, 0)
    outs = call(
        second_pieces,
        [((72, width), F32)] * 4 + [((64, width), F32)] * 4,
        pos,
        a0,
        ar,
        al,
        b0,
        br,
        bl,
        smem=1,
    )
    sa, sb = outs[:4], outs[4:]
    ra, rb = [], []
    for d in (1, 2, 3):
        ra.append(shift_dp(sa[d], 0, d, 0))
        rb.append(shift_dp(sb[d], d, 0, 0))
    scale = (1.0 / total_cents) * (total_cents / total_rows)
    new, mass = call(
        functools.partial(finish, scale),
        [((128, width), F32), ((1, 128), F32)],
        pos,
        v,
        sa[0],
        *ra,
        sb[0],
        *rb,
        smem=1,
    )
    return new, mass.reshape(128)


def solution(mesh):
    in_specs = (P("dp", None), P("cent", None))
    out_specs = (P(("cent", "dp"), None), P(("cent", "dp")))
    return jax.shard_map(local, mesh=mesh, in_specs=in_specs, out_specs=out_specs, check_vma=False)
```

```python
import functools

import jax
import jax.numpy as jnp
from jax import lax
from jax.experimental import pallas as pl
from jax.experimental.pallas import tpu as pltpu
from jax.sharding import PartitionSpec as P

ITERS = 3
TAU = 0.02
NX, NZ, NC, NY = 4, 4, 2, 4
F32, BF16 = jnp.float32, jnp.bfloat16
VM = pltpu.VMEM
LIMIT = 16 * 1024 * 1024
BLK = 256


def index(x, z, c):
    return (x * NZ + z) * NC + c


def permute(value, target):
    pairs = [
        (index(x, z, c), index(*target(x, z, c)))
        for x in range(NX)
        for z in range(NZ)
        for c in range(NC)
    ]
    return lax.ppermute(value, "dp", pairs)


def other_core(value):
    return permute(value, lambda x, z, c: (x, z, 1 - c))


def first_axis(value, d):
    def target(x, z, c):
        return ((x + d) % NX, z, c) if c == 0 else (x, (z + d) % NZ, c)

    return permute(value, target)


def second_axis(value, d):
    def target(x, z, c):
        return (x, (z + d) % NZ, c) if c == 0 else ((x + d) % NX, z, c)

    return permute(value, target)


def along_x(value, d):
    return permute(value, lambda x, z, c: ((x + d) % NX, z, c))


def along_z(value, d):
    return permute(value, lambda x, z, c: (x, (z + d) % NZ, c))


def shift_y(value, d):
    return lax.ppermute(value, "cent", [(i, (i + d) % NY) for i in range(NY)])


def flip_y(value, bit):
    return lax.ppermute(value, "cent", [(i, i ^ bit) for i in range(NY)])


def place():
    dp = lax.axis_index("dp")
    core = lax.rem(dp, NC)
    z = lax.rem(lax.div(dp, NC), NZ)
    x = lax.div(dp, NC * NZ)
    flip = core == 1
    first = (jnp.where(flip, z, x), jnp.where(flip, 1, NZ))
    second = (jnp.where(flip, x, z), jnp.where(flip, NZ, 1))
    return x, z, core, first, second


HBM, HERE, PINNED = "hbm", "vmem", "pinned"


def call(body, outs, *args, cost=None, **kw):
    spaces = {HBM: pltpu.HBM, HERE: VM, PINNED: VM}
    if cost:
        kw["cost_estimate"] = pl.CostEstimate(flops=cost, bytes_accessed=1 << 20, transcendentals=0)
    return pl.pallas_call(
        body,
        in_specs=[pl.BlockSpec(memory_space=spaces[p]) for _, p in args],
        out_specs=[pl.BlockSpec(memory_space=VM) for _ in outs],
        out_shape=[
            VM(s, d) if p == PINNED else jax.ShapeDtypeStruct(s, d) for s, d, p in outs
        ],
        compiler_params=pltpu.CompilerParams(vmem_limit_bytes=LIMIT),
        **kw,
    )(*[pltpu.with_memory_space_constraint(a, VM) if p == PINNED else a for a, p in args])


def norm_rows(wide):
    mean = jnp.mean(wide * wide, axis=1, keepdims=True)
    return wide * lax.rsqrt(mean + 1e-06)


def normalize(emb_ref, wide_ref, xh_ref):
    xh = norm_rows(emb_ref[...].astype(F32)).astype(BF16)
    xh_ref[...] = xh
    wide_ref[...] = xh.astype(F32)


def lane_total(acc_ref):
    ones = jnp.ones((8, 128), F32)
    total = lax.dot_general(
        ones,
        acc_ref[...],
        (((1,), (1,)), ((), ())),
        precision=lax.Precision.HIGHEST,
        preferred_element_type=F32,
    )
    return total[0:1, :]


def fold_lanes(block):
    total = block[:, 0:128]
    for t in range(1, block.shape[1] // 128):
        total = total + block[:, t * 128 : (t + 1) * 128]
    return total


def fold_rows(block):
    return jnp.sum(block.reshape(block.shape[0] // 8, 8, block.shape[1]), axis=0)


def scores_exp(ch, xh):
    width = xh.shape[1]
    scores = lax.dot_general(ch, xh, (((1,), (1,)), ((), ())), preferred_element_type=F32)
    return jnp.exp(scores * (1.0 / (TAU * width)))


def energy_own(cents_ref, xh_ref, et_ref, ch_ref, acc_ref, r_ref, raw_ref, sems):
    core = place()[2]
    n_blocks = ch_ref.shape[0] // BLK
    parts = BLK // 128

    def fetch(i):
        return pltpu.make_async_copy(
            cents_ref.at[pl.ds(i * parts, parts), core], raw_ref.at[i], sems.at[i]
        )

    for i in range(n_blocks):
        fetch(i).start()
    r_acc = jnp.zeros((8, xh_ref.shape[0]), F32)
    for i in range(n_blocks):
        rows = slice(i * BLK, (i + 1) * BLK)
        fetch(i).wait()
        raw = raw_ref[i].astype(F32).reshape(BLK, ch_ref.shape[1])
        ch = norm_rows(raw).astype(BF16)
        ch_ref[rows, :] = ch
        e = scores_exp(ch, xh_ref[...])
        et_ref[rows, :] = e
        acc_ref[rows, :] = fold_lanes(e)
        r_acc = r_acc + fold_rows(e)
    r_ref[...] = jnp.sum(r_acc, axis=0, keepdims=True)


def energy_peer(ch_ref, wide_ref, acc_ref, r_own_ref, et_ref, xh_ref, r_ref, s_ref, c_ref, tot_ref):
    n_blocks = ch_ref.shape[0] // BLK
    half = xh_ref.shape[0]
    xh_ref[...] = wide_ref[...].astype(BF16)
    r_acc = jnp.zeros((8, half), F32)
    for i in range(n_blocks):
        rows = slice(i * BLK, (i + 1) * BLK)
        e = scores_exp(ch_ref[rows, :], xh_ref[...])
        et_ref[rows, :] = e
        tot_ref[rows, :] = acc_ref[rows, :] + fold_lanes(e)
        r_acc = r_acc + fold_rows(e)
    r_peer = jnp.sum(r_acc, axis=0, keepdims=True)
    r_ref[:, 0:half] = r_own_ref[...]
    r_ref[:, half:] = r_peer
    s_ref[:, 0:half] = r_peer
    s_ref[:, half:] = r_own_ref[...]
    c_ref[...] = lane_total(tot_ref)


def new_u(u_ref, r_refs):
    r = r_refs[0][...] + r_refs[1][...]
    for ref in r_refs[2:]:
        r = r + ref[...]
    return jnp.sqrt(u_ref[...] / r)


def spread_block(row):
    return jnp.broadcast_to(row, (128, 128)).T


def scale_pass(ratio, *refs):
    (eta_ref, etb_ref, u_ref, v_ref, r0, r1, c0, c1, c2, c3) = refs[:10]
    (uo_ref, vo_ref, ro_ref, so_ref, co_ref, vcol_ref, acc_ref) = refs[10:]
    u = new_u(u_ref, (r0, r1))
    c = (c0[...] + c1[...]) + (c2[...] + c3[...])
    v = jnp.sqrt(v_ref[...] * ratio / c)
    uo_ref[...] = u
    vo_ref[...] = v
    for t in range(v.shape[1] // 128):
        block = slice(t * 128, (t + 1) * 128)
        vcol_ref[block, :] = spread_block(v[:, block])
    half = eta_ref.shape[1]
    tiles = half // 128
    ub = [jnp.broadcast_to(u[:, t * 128 : (t + 1) * 128], (8, 128)) for t in range(2 * tiles)]

    def step(i, carry):
        rows = pl.ds(pl.multiple_of(i * 8, 8), 8)
        vb = vcol_ref[rows, :]
        out, parts = [], []
        for t in range(2 * tiles):
            ref = eta_ref if t < tiles else etb_ref
            e = ref[rows, (t % tiles) * 128 : (t % tiles + 1) * 128]
            out.append(carry[t] + e * vb)
            parts.append(e * ub[t])
        while len(parts) > 1:
            parts = [a + b for a, b in zip(parts[::2], parts[1::2])]
        acc_ref[rows, :] = parts[0]
        return tuple(out)

    zero = jnp.zeros((8, 128), F32)
    acc = lax.fori_loop(0, eta_ref.shape[0] // 8, step, (zero,) * (2 * tiles), unroll=4)
    for t in range(2 * tiles):
        total = jnp.sum(acc[t], axis=0, keepdims=True)
        swapped = (t + tiles) % (2 * tiles)
        ro_ref[:, t * 128 : (t + 1) * 128] = total
        so_ref[:, swapped * 128 : (swapped + 1) * 128] = total
    co_ref[...] = lane_total(acc_ref)


def weigh(d, upper, out_ref, eta_ref, etb_ref, xa_ref, xb_ref, ku_ref, c_ref):
    (at, stride), (_, step) = place()[3:]
    begin = lax.rem(at + d, 4) * stride
    half = eta_ref.shape[1]
    ones = jnp.ones((8, 128), F32)
    out_ref[256:264, :] = jnp.zeros((8, 512), F32)
    parts = ([], [])
    for k in range(4):
        start = pl.multiple_of((begin + k * step) * 128, 128)
        rows = pl.ds(pl.multiple_of(start + 64 * upper, 64), 64)
        total = jnp.zeros((64, 128), F32)
        for peer, ref in ((False, eta_ref), (True, etb_ref)):
            tiles = []
            for t in range(half // 128):
                lanes = slice(t * 128, (t + 1) * 128)
                ku = ku_ref[:, half * peer + t * 128 : half * peer + (t + 1) * 128]
                scaled = ku * ref[rows, lanes]
                total = total + scaled
                tiles.append(scaled.astype(BF16))
            parts[peer].append(jnp.concatenate(tiles, axis=1))
        mass = lax.dot_general(
            ones,
            total,
            (((1,), (1,)), ((), ())),
            precision=lax.Precision.HIGHEST,
            preferred_element_type=F32,
        )
        lanes = slice(k * 128 + 64 * upper, k * 128 + 64 * upper + 64)
        out_ref[256:257, lanes] = mass[0:1, :]
        if not upper:
            out_ref[257:258, k * 128 : (k + 1) * 128] = c_ref[:, pl.ds(start, 128)]
    out_ref[0:256, :] = jnp.dot(
        jnp.concatenate(parts[0], axis=0), xa_ref[...], preferred_element_type=F32
    ) + jnp.dot(jnp.concatenate(parts[1], axis=0), xb_ref[...], preferred_element_type=F32)


def plan_first(big, eta, etb, xa, xb, c_ref, u_ref, r0, r1, r2, r3, ku_ref, low_ref, high_ref):
    ku_ref[...] = big * new_u(u_ref, (r0, r1, r2, r3))
    weigh(2, 0, low_ref, eta, etb, xa, xb, ku_ref, c_ref)
    weigh(2, 1, high_ref, eta, etb, xa, xb, ku_ref, c_ref)


def plan_more(low_d, high_d, *refs):
    weigh(low_d, 0, refs[-2], *refs[:6])
    weigh(high_d, 1, refs[-1], *refs[:6])


def add_transit(a, b, c, d, out0, out1):
    out0[...] = a[...] + b[...]
    out1[...] = c[...] + d[...]


def second_pieces(low0, low1, low3, high0, high1, high3, *outs):
    at = place()[4][0]
    for d in range(4):
        k = lax.rem(at + d, 4)
        rows = pl.ds(pl.multiple_of(k * 64, 64), 64)
        lanes = pl.ds(pl.multiple_of(k * 128, 128), 128)
        outs[d][0:64, :] = low0[rows, :] + low1[rows, :] + low3[rows, :]
        outs[d][64:128, :] = high0[rows, :] + high1[rows, :] + high3[rows, :]
        low = low0[256:264, lanes] + low1[256:264, lanes] + low3[256:264, lanes]
        high = high0[256:264, lanes] + high1[256:264, lanes] + high3[256:264, lanes]
        outs[d][128:136, 0:128] = low + high
        outs[d][128:136, 128:] = jnp.zeros((8, 384), F32)


def finish(ratio, scale, v_ref, a, b, c, d, new_ref, mass_ref):
    x, z = place()[:2]
    w = (a[...] + b[...]) + (c[...] + d[...])
    v = v_ref[:, pl.ds(pl.multiple_of((x * NZ + z) * 128, 128), 128)]
    v = jnp.sqrt(v * ratio / w[129:130, 0:128])
    mass_ref[...] = v * (w[128:129, 0:128] * scale)
    spread = spread_block(v)
    new_ref[...] = norm_rows(w[0:128, :] * jnp.concatenate([spread] * 4, axis=1))


def local(embeddings, centroids):
    rows, width = embeddings.shape
    all_cents = centroids.shape[0]
    n = all_cents // NC
    both = 2 * rows
    total_rows = float(rows * lax.axis_size("dp"))
    total_cents = float(all_cents * lax.axis_size("cent"))
    ratio = total_rows / total_cents
    tile = 2 * n * rows * width

    block = pl.BlockSpec((256, width), lambda i: (i, 0))
    wide, xa = pl.pallas_call(
        normalize,
        grid=(rows // 256,),
        in_specs=[block],
        out_specs=[block, block],
        out_shape=[
            jax.ShapeDtypeStruct((rows, width), F32),
            jax.ShapeDtypeStruct((rows, width), BF16),
        ],
        compiler_params=pltpu.CompilerParams(vmem_limit_bytes=LIMIT),
    )(embeddings)
    wide_peer = other_core(wide)
    eta, ch, acc, r_own = call(
        energy_own,
        [
            ((n, rows), F32, PINNED),
            ((n, width), BF16, HERE),
            ((n, 128), F32, HERE),
            ((1, rows), F32, HERE),
        ],
        (centroids.reshape(n // 128, NC, 128, width), HBM),
        (xa, HERE),
        scratch_shapes=[
            VM((n // BLK, BLK // 128, 128, width), BF16),
            pltpu.SemaphoreType.DMA((n // BLK,)),
        ],
        cost=2 * tile,
    )
    sums = [((1, both), F32, HERE), ((1, both), F32, HERE), ((1, n), F32, HERE)]
    etb, xb, r, swapped, c = call(
        energy_peer,
        [((n, rows), F32, PINNED), ((rows, width), BF16, HERE), *sums],
        (ch, HERE),
        (wide_peer, HERE),
        (acc, HERE),
        (r_own, HERE),
        scratch_shapes=[VM((n, 128), F32)],
        cost=2 * tile,
    )
    u = jnp.ones((1, both), F32)
    v = jnp.ones((1, n), F32)
    for step in range(ITERS - 1):
        r = r + other_core(swapped)
        cx = [along_x(c, d) for d in (1, 2, 3)]
        ry = flip_y(r, 1)
        c = (c + cx[0]) + (cx[1] + cx[2])
        r = r + ry
        cz = [along_z(c, d) for d in (1, 2, 3)]
        ry = flip_y(r, 2)
        u, v, r, swapped, c = call(
            functools.partial(scale_pass, ratio),
            [((1, both), F32, HERE), ((1, n), F32, HERE), *sums],
            (eta, PINNED),
            (etb, PINNED),
            *[(a, HERE) for a in (u, v, r, ry, c, *cz)],
            scratch_shapes=[VM((n, 128), F32)] * 2,
            cost=2 * tile,
        )
    r = r + other_core(swapped)
    piece = ((264, width), F32, HERE)
    ku, low2, high2 = call(
        functools.partial(plan_first, total_cents),
        [((1, both), F32, HERE), piece, piece],
        (eta, PINNED),
        (etb, PINNED),
        *[(a, HERE) for a in (xa, xb, c, u, r, *[shift_y(r, d) for d in (1, 2, 3)])],
        cost=tile,
    )
    from_left = first_axis(low2, 1)
    from_right = first_axis(high2, 3)

    def plan(low_d, high_d, after):
        return call(
            functools.partial(plan_more, low_d, high_d),
            [piece] * 2,
            (eta, PINNED),
            (etb, PINNED),
            *[(a, HERE) for a in (xa, xb, ku, c)],
            (after, HBM),
            cost=tile,
        )

    low3, high1 = plan(3, 1, ku)
    high_l = first_axis(high1, 1)
    low_r = first_axis(low3, 3)
    low1, high3 = plan(1, 3, low3)
    low0, high0 = plan(0, 0, low1)
    low1, high3 = call(
        add_transit,
        [piece] * 2,
        *[(a, HERE) for a in (low1, from_left, high3, from_right)],
    )
    low_l = first_axis(low1, 1)
    high_r = first_axis(high3, 3)
    pieces = call(
        second_pieces,
        [((136, width), F32, HERE)] * 4,
        *[(a, HERE) for a in (low0, low_l, low_r, high0, high_l, high_r)],
    )
    got = [second_axis(pieces[d], d) for d in (1, 2, 3)]
    scale = (1.0 / total_cents) * (total_cents / total_rows)
    new, mass = call(
        functools.partial(finish, ratio, scale),
        [((128, width), F32, HERE), ((1, 128), F32, HERE)],
        *[(a, HERE) for a in (v, pieces[0], *got)],
    )
    return new, mass.reshape(128)


def solution(mesh):
    in_specs = (P("dp", None), P("cent", None))
    out_specs = (P(("cent", "dp"), None), P(("cent", "dp")))
    return jax.shard_map(local, mesh=mesh, in_specs=in_specs, out_specs=out_specs, check_vma=False)
```

```python
import functools

import jax
import jax.numpy as jnp
from jax import lax
from jax.experimental import pallas as pl
from jax.experimental.pallas import tpu as pltpu
from jax.sharding import PartitionSpec as P

TAU = 0.02
NX, NZ, NC, NY = 4, 4, 2, 4
F32, BF16 = jnp.float32, jnp.bfloat16
VM = pltpu.VMEM
LIMIT = 16 * 1024 * 1024
BLK = 256


def index(x, z, c):
    return (x * NZ + z) * NC + c


def permute(value, target):
    pairs = [
        (index(x, z, c), index(*target(x, z, c)))
        for x in range(NX)
        for z in range(NZ)
        for c in range(NC)
    ]
    return lax.ppermute(value, "dp", pairs)


def other_core(value):
    return permute(value, lambda x, z, c: (x, z, 1 - c))


def first_axis(value, d):
    return permute(value, lambda x, z, c: (x ^ d, z, c) if c == 0 else (x, z ^ d, c))


def second_axis(value, d):
    return permute(value, lambda x, z, c: (x, z ^ d, c) if c == 0 else (x ^ d, z, c))


def flip_x(value, bit):
    return permute(value, lambda x, z, c: (x ^ bit, z, c))


def flip_z(value, bit):
    return permute(value, lambda x, z, c: (x, z ^ bit, c))


def flip_y(value, bit):
    return lax.ppermute(value, "cent", [(i, i ^ bit) for i in range(NY)])


def place():
    dp = lax.axis_index("dp")
    core = lax.rem(dp, NC)
    z = lax.rem(lax.div(dp, NC), NZ)
    x = lax.div(dp, NC * NZ)
    flip = core == 1
    first = (jnp.where(flip, z, x), jnp.where(flip, 1, NZ))
    second = (jnp.where(flip, x, z), jnp.where(flip, NZ, 1))
    return x, z, core, first, second


def hbm(value):
    return pltpu.with_memory_space_constraint(value, pltpu.HBM)


HBM, LATER, HERE, PINNED = "hbm", "later", "vmem", "pinned"


def call(body, outs, *args, cost=None, **kw):
    spaces = {HBM: pltpu.HBM, LATER: pltpu.HBM, HERE: VM, PINNED: VM}
    if cost:
        kw["cost_estimate"] = pl.CostEstimate(flops=cost, bytes_accessed=1 << 20, transcendentals=0)
    return pl.pallas_call(
        body,
        in_specs=[pl.BlockSpec(memory_space=spaces[p]) for _, p in args],
        out_specs=[pl.BlockSpec(memory_space=VM) for _ in outs],
        out_shape=[
            VM(s, d) if p == PINNED else jax.ShapeDtypeStruct(s, d) for s, d, p in outs
        ],
        compiler_params=pltpu.CompilerParams(vmem_limit_bytes=LIMIT),
        **kw,
    )(*[pltpu.with_memory_space_constraint(a, VM) if p == PINNED else a for a, p in args])


def norm_rows(wide):
    mean = jnp.mean(wide * wide, axis=1, keepdims=True)
    return wide * lax.rsqrt(mean + 1e-06)


def normalize(emb_ref, wide_ref, xh_ref, raw_ref, sems):
    n_parts, size = raw_ref.shape[:2]

    def fetch(i):
        return pltpu.make_async_copy(
            emb_ref.at[pl.ds(i * size, size)], raw_ref.at[i], sems.at[i]
        )

    for i in range(n_parts):
        fetch(i).start()
    for i in range(n_parts):
        rows = slice(i * size, (i + 1) * size)
        fetch(i).wait()
        xh = norm_rows(raw_ref[i].astype(F32)).astype(BF16)
        xh_ref[rows, :] = xh
        wide_ref[rows, :] = xh.astype(F32)


def lane_total(block):
    return jnp.sum(block.T, axis=0, keepdims=True)


def lane_totals(acc_ref, out_ref):
    for t in range(acc_ref.shape[0] // 128):
        block = slice(t * 128, (t + 1) * 128)
        out_ref[:, block] = lane_total(acc_ref[block, :])


def fold_lanes(block):
    total = block[:, 0:128]
    for t in range(1, block.shape[1] // 128):
        total = total + block[:, t * 128 : (t + 1) * 128]
    return total


def fold_rows(block):
    return jnp.sum(block.reshape(block.shape[0] // 8, 8, block.shape[1]), axis=0)


def scores_exp(ch, xh):
    width = xh.shape[1]
    scores = lax.dot_general(ch, xh, (((1,), (1,)), ((), ())), preferred_element_type=F32)
    return jnp.exp(scores * (1.0 / (TAU * width)))


def energy_own(cents_ref, xh_ref, et_ref, ch_ref, acc_ref, r_ref, raw_ref, sems):
    core = place()[2]
    n_blocks = ch_ref.shape[0] // BLK
    parts = BLK // 128

    def fetch(i):
        return pltpu.make_async_copy(
            cents_ref.at[pl.ds(i * parts, parts), core], raw_ref.at[i], sems.at[i]
        )

    for i in range(n_blocks):
        fetch(i).start()
    def prepare(i):
        fetch(i).wait()
        raw = raw_ref[i].astype(F32).reshape(BLK, ch_ref.shape[1])
        ch_ref[i * BLK : (i + 1) * BLK, :] = norm_rows(raw).astype(BF16)

    prepare(0)
    r_acc = jnp.zeros((8, xh_ref.shape[0]), F32)
    for i in range(n_blocks):
        rows = slice(i * BLK, (i + 1) * BLK)
        if i + 1 < n_blocks:
            prepare(i + 1)
        e = scores_exp(ch_ref[rows, :], xh_ref[...])
        et_ref[rows, :] = e
        acc_ref[rows, :] = fold_lanes(e)
        r_acc = r_acc + fold_rows(e)
    r_ref[...] = jnp.sum(r_acc, axis=0, keepdims=True)


def energy_peer(ch_ref, wide_ref, acc_ref, r_own_ref, et_ref, xh_ref, r_ref, s_ref, c_ref, tot_ref):
    n_blocks = ch_ref.shape[0] // BLK
    half = xh_ref.shape[0]
    xh_ref[...] = wide_ref[...].astype(BF16)
    r_acc = jnp.zeros((8, half), F32)
    for i in range(n_blocks):
        rows = slice(i * BLK, (i + 1) * BLK)
        e = scores_exp(ch_ref[rows, :], xh_ref[...])
        et_ref[rows, :] = e
        tot_ref[rows, :] = acc_ref[rows, :] + fold_lanes(e)
        r_acc = r_acc + fold_rows(e)
    r_peer = jnp.sum(r_acc, axis=0, keepdims=True)
    r_ref[:, 0:half] = r_own_ref[...]
    r_ref[:, half:] = r_peer
    s_ref[:, 0:half] = r_peer
    s_ref[:, half:] = r_own_ref[...]
    lane_totals(tot_ref, c_ref)


def total_of(refs, block):
    total = refs[0][:, block]
    for ref in refs[1:]:
        total = total + ref[:, block]
    return total


def spread_block(row):
    return jnp.broadcast_to(row, (128, 128)).T


def column_pass(n_parts, eta_ref, etb_ref, first_c_ref, *refs):
    uo_ref, co_ref, acc_ref = refs[n_parts:]
    n = eta_ref.shape[0]
    u = jnp.sqrt(1.0 / total_of(refs[:n_parts], slice(None)))
    uo_ref[...] = u
    co_ref[:, 0:n] = first_c_ref[...]
    tiles = eta_ref.shape[1] // 128
    ub = [jnp.broadcast_to(u[:, t * 128 : (t + 1) * 128], (8, 128)) for t in range(2 * tiles)]

    def step(i, carry):
        rows = pl.ds(pl.multiple_of(i * 8, 8), 8)
        parts = []
        for t in range(2 * tiles):
            ref = eta_ref if t < tiles else etb_ref
            parts.append(ref[rows, (t % tiles) * 128 : (t % tiles + 1) * 128] * ub[t])
        while len(parts) > 1:
            parts = [a + b for a, b in zip(parts[::2], parts[1::2])]
        acc_ref[rows, :] = parts[0]
        return carry

    lax.fori_loop(0, n // 8, step, 0, unroll=8)
    for t in range(n // 128):
        block = slice(t * 128, (t + 1) * 128)
        co_ref[:, n + t * 128 : n + (t + 1) * 128] = lane_total(acc_ref[block, :])


def row_pass(n_parts, ratio, eta_ref, etb_ref, *refs):
    vo_ref, ro_ref, so_ref, one_ref, two_ref = refs[n_parts:]
    n = eta_ref.shape[0]
    v1 = jnp.sqrt(ratio / total_of(refs[:n_parts], slice(0, n)))
    v2 = jnp.sqrt(v1 * ratio / total_of(refs[:n_parts], slice(n, 2 * n)))
    vo_ref[...] = v2
    for t in range(n // 128):
        block = slice(t * 128, (t + 1) * 128)
        one_ref[block, :] = spread_block(v1[:, block])
        two_ref[block, :] = spread_block(v2[:, block])
    tiles = eta_ref.shape[1] // 128
    zero = jnp.zeros((8, 128), F32)
    for h, ref in ((0, eta_ref), (1, etb_ref)):

        def step(i, carry):
            rows = pl.ds(pl.multiple_of(i * 8, 8), 8)
            b1, b2 = one_ref[rows, :], two_ref[rows, :]
            out1, out2 = [], []
            for t in range(tiles):
                e = ref[rows, t * 128 : (t + 1) * 128]
                out1.append(carry[t] + e * b1)
                out2.append(carry[tiles + t] + e * b2)
            return (*out1, *out2)

        acc = lax.fori_loop(0, n // 8, step, (zero,) * (2 * tiles), unroll=8)
        for t in range(2 * tiles):
            total = jnp.sum(acc[t], axis=0, keepdims=True)
            at = (t // tiles * 2 + h) * tiles + t % tiles
            swapped = (t // tiles * 2 + 1 - h) * tiles + t % tiles
            ro_ref[:, at * 128 : (at + 1) * 128] = total
            so_ref[:, swapped * 128 : (swapped + 1) * 128] = total


def weigh(d, upper, out_ref, eta_ref, etb_ref, xa_ref, xb_ref, ku_ref, u2_ref):
    (at, stride), (_, step) = place()[3:]
    begin = (at ^ d) * stride
    half = eta_ref.shape[1]
    out_ref[256:264, :] = jnp.zeros((8, 512), F32)
    parts = ([], [])
    for k in range(4):
        start = (begin + k * step) * 128 + 64 * upper
        rows = pl.ds(pl.multiple_of(start, 64), 64)
        total = jnp.zeros((64, 128), F32)
        second = jnp.zeros((64, 128), F32)
        for peer, ref in ((False, eta_ref), (True, etb_ref)):
            tiles = []
            for t in range(half // 128):
                lanes = slice(t * 128, (t + 1) * 128)
                at_u = slice(half * peer + t * 128, half * peer + (t + 1) * 128)
                e = ref[rows, lanes]
                scaled = ku_ref[:, at_u] * e
                total = total + scaled
                second = second + u2_ref[:, at_u] * e
                tiles.append(scaled.astype(BF16))
            parts[peer].append(jnp.concatenate(tiles, axis=1))
        lanes = slice(k * 128 + 64 * upper, k * 128 + 64 * upper + 64)
        out_ref[256:257, lanes] = lane_total(total)
        out_ref[257:258, lanes] = lane_total(second)
    out_ref[0:256, :] = jnp.dot(
        jnp.concatenate(parts[0], axis=0), xa_ref[...], preferred_element_type=F32
    ) + jnp.dot(jnp.concatenate(parts[1], axis=0), xb_ref[...], preferred_element_type=F32)


def plan_first(n_parts, big, eta, etb, xa, xb, u_ref, *refs):
    ku_ref, u2_ref, low_ref = refs[n_parts:]
    both = u_ref.shape[1]
    u2 = jnp.sqrt(u_ref[...] / total_of(refs[:n_parts], slice(0, both)))
    u2_ref[...] = u2
    ku_ref[...] = big * jnp.sqrt(u2 / total_of(refs[:n_parts], slice(both, 2 * both)))
    weigh(2, 0, low_ref, eta, etb, xa, xb, ku_ref, u2_ref)


def plan_more(which, *refs):
    for (d, upper), out_ref in zip(which, refs[7:]):
        weigh(d, upper, out_ref, *refs[:6])


def plan_on(d, upper, *refs):
    weigh(d, upper, refs[-1], *refs[:6])
    refs[-1][...] += refs[7][...]


def second_pieces(low0, low1, low3, high0, high1, high3, *outs):
    at = place()[4][0]
    for d in range(4):
        k = at ^ d
        rows = pl.ds(pl.multiple_of(k * 64, 64), 64)
        lanes = pl.ds(pl.multiple_of(k * 128, 128), 128)
        outs[d][0:64, :] = low0[rows, :] + low1[rows, :] + low3[rows, :]
        outs[d][64:128, :] = high0[rows, :] + high1[rows, :] + high3[rows, :]
        low = low0[256:264, lanes] + low1[256:264, lanes] + low3[256:264, lanes]
        high = high0[256:264, lanes] + high1[256:264, lanes] + high3[256:264, lanes]
        outs[d][128:136, 0:128] = low + high
        outs[d][128:136, 128:] = jnp.zeros((8, 384), F32)


def finish(ratio, scale, v_ref, a, b, c, d, new_ref, mass_ref):
    x, z = place()[:2]
    w = (a[...] + b[...]) + (c[...] + d[...])
    v = v_ref[:, pl.ds(pl.multiple_of((x * NZ + z) * 128, 128), 128)]
    v = jnp.sqrt(v * ratio / w[129:130, 0:128])
    mass_ref[...] = v * (w[128:129, 0:128] * scale)
    spread = spread_block(v)
    new_ref[...] = norm_rows(w[0:128, :] * jnp.concatenate([spread] * 4, axis=1))


def local(embeddings, centroids):
    rows, width = embeddings.shape
    all_cents = centroids.shape[0]
    n = all_cents // NC
    both = 2 * rows
    total_rows = float(rows * lax.axis_size("dp"))
    total_cents = float(all_cents * lax.axis_size("cent"))
    ratio = total_rows / total_cents
    tile = 2 * n * rows * width

    wide, xa = call(
        normalize,
        [((rows, width), F32, HERE), ((rows, width), BF16, HERE)],
        (hbm(embeddings), HBM),
        scratch_shapes=[VM((8, rows // 8, width), BF16), pltpu.SemaphoreType.DMA((8,))],
    )
    wide_peer = other_core(wide)
    eta, ch, acc, r_own = call(
        energy_own,
        [
            ((n, rows), F32, PINNED),
            ((n, width), BF16, HERE),
            ((n, 128), F32, HERE),
            ((1, rows), F32, HERE),
        ],
        (hbm(centroids.reshape(n // 128, NC, 128, width)), HBM),
        (xa, HERE),
        scratch_shapes=[
            VM((n // BLK, BLK // 128, 128, width), BF16),
            pltpu.SemaphoreType.DMA((n // BLK,)),
        ],
        cost=2 * tile,
    )
    vec_u = ((1, both), F32, HERE)
    vec_v = ((1, n), F32, HERE)
    etb, xb, r, swapped, c = call(
        energy_peer,
        [((n, rows), F32, PINNED), ((rows, width), BF16, HERE), vec_u, vec_u, vec_v],
        (ch, HERE),
        (wide_peer, HERE),
        (acc, HERE),
        (r_own, HERE),
        scratch_shapes=[VM((n, 128), F32)],
        cost=2 * tile,
    )
    tiles_of_e = ((eta, PINNED), (etb, PINNED))

    def over_rows(c):
        x = [flip_x(c, d) for d in (2, 1, 3)]
        c = (c + x[0]) + (x[1] + x[2])
        return [c, *[flip_z(c, d) for d in (2, 1, 3)]]

    def over_centroids(r, swapped):
        r = r + other_core(swapped)
        return [r, *[flip_y(r, d) for d in (2, 1, 3)]]

    parts = over_centroids(r, swapped)
    u, c = call(
        functools.partial(column_pass, len(parts)),
        [vec_u, ((1, 2 * n), F32, HERE)],
        *tiles_of_e,
        *[(a, HERE) for a in (c, *parts)],
        scratch_shapes=[VM((n, 128), F32)],
        cost=tile // 2,
    )
    parts = over_rows(c)
    v, r, swapped = call(
        functools.partial(row_pass, len(parts), ratio),
        [vec_v, ((1, 2 * both), F32, HERE), ((1, 2 * both), F32, HERE)],
        *tiles_of_e,
        *[(a, HERE) for a in parts],
        scratch_shapes=[VM((n, 128), F32)] * 2,
        cost=tile,
    )
    parts = over_centroids(r, swapped)
    piece = ((264, width), F32, HERE)
    ku, u2, low2 = call(
        functools.partial(plan_first, len(parts), total_cents),
        [vec_u, vec_u, piece],
        *tiles_of_e,
        *[(a, HERE) for a in (xa, xb, u, *parts)],
        cost=tile // 2,
    )
    from_a = first_axis(low2, 1)
    base = (*tiles_of_e, *[(a, HERE) for a in (xa, xb, ku, u2)])

    def plan(which, after):
        return call(
            functools.partial(plan_more, which),
            [piece] * len(which),
            *base,
            (after, LATER),
            cost=tile * len(which) // 2,
        )

    def plan_sum(d, upper, got, after):
        return call(
            functools.partial(plan_on, d, upper),
            [piece],
            *base,
            (after, LATER),
            (got, HERE),
            cost=tile // 2,
        )[0]

    (high2,) = plan(((2, 1),), low2)
    from_b = first_axis(high2, 3)
    (low1,) = plan(((1, 0),), high2)
    low_a = first_axis(low1, 1)
    (high3,) = plan(((3, 1),), low1)
    high_b = first_axis(high3, 3)
    low0, high0 = plan(((0, 0), (0, 1)), high3)
    low3 = plan_sum(3, 0, from_a, low0)
    low_b = first_axis(low3, 3)
    high1 = plan_sum(1, 1, from_b, low3)
    high_a = first_axis(high1, 1)
    pieces = call(
        second_pieces,
        [((136, width), F32, HERE)] * 4,
        *[(a, HERE) for a in (low0, low_a, low_b, high0, high_a, high_b)],
    )
    got = [second_axis(pieces[d], d) for d in (1, 2, 3)]
    scale = (1.0 / total_cents) * (total_cents / total_rows)
    new, mass = call(
        functools.partial(finish, ratio, scale),
        [((128, width), F32, HERE), ((1, 128), F32, HERE)],
        *[(a, HERE) for a in (v, pieces[0], *got)],
    )
    return new, mass.reshape(128)


def solution(mesh):
    in_specs = (P("dp", None), P("cent", None))
    out_specs = (P(("cent", "dp"), None), P(("cent", "dp")))
    return jax.shard_map(local, mesh=mesh, in_specs=in_specs, out_specs=out_specs, check_vma=False)
```

```python
import functools

import jax
import jax.numpy as jnp
from jax import lax
from jax.experimental import pallas as pl
from jax.experimental.pallas import tpu as pltpu
from jax.sharding import PartitionSpec as P

TAU = 0.02
NX, NZ, NC, NY = 4, 4, 2, 4
F32, BF16 = jnp.float32, jnp.bfloat16
VM = pltpu.VMEM
LIMIT = 16 * 1024 * 1024
BLK = 256


def index(x, z, c):
    return (x * NZ + z) * NC + c


def permute(value, target):
    pairs = [
        (index(x, z, c), index(*target(x, z, c)))
        for x in range(NX)
        for z in range(NZ)
        for c in range(NC)
    ]
    return lax.ppermute(value, "dp", pairs)


def other_core(value):
    return permute(value, lambda x, z, c: (x, z, 1 - c))


def first_axis(value, d):
    return permute(value, lambda x, z, c: (x ^ d, z, c) if c == 0 else (x, z ^ d, c))


def second_axis(value, d):
    return permute(value, lambda x, z, c: (x, z ^ d, c) if c == 0 else (x ^ d, z, c))


def flip_x(value, bit):
    return permute(value, lambda x, z, c: (x ^ bit, z, c))


def flip_z(value, bit):
    return permute(value, lambda x, z, c: (x, z ^ bit, c))


def flip_y(value, bit):
    return lax.ppermute(value, "cent", [(i, i ^ bit) for i in range(NY)])


def place():
    dp = lax.axis_index("dp")
    core = lax.rem(dp, NC)
    z = lax.rem(lax.div(dp, NC), NZ)
    x = lax.div(dp, NC * NZ)
    flip = core == 1
    first = (jnp.where(flip, z, x), jnp.where(flip, 1, NZ))
    second = (jnp.where(flip, x, z), jnp.where(flip, NZ, 1))
    return x, z, core, first, second


def hbm(value):
    return pltpu.with_memory_space_constraint(value, pltpu.HBM)


HBM, LATER, HERE, PINNED = "hbm", "later", "vmem", "pinned"


def call(body, outs, *args, cost=None, **kw):
    spaces = {HBM: pltpu.HBM, LATER: pltpu.HBM, HERE: VM, PINNED: VM}
    if cost:
        kw["cost_estimate"] = pl.CostEstimate(flops=cost, bytes_accessed=1 << 20, transcendentals=0)
    return pl.pallas_call(
        body,
        in_specs=[pl.BlockSpec(memory_space=spaces[p]) for _, p in args],
        out_specs=[pl.BlockSpec(memory_space=VM) for _ in outs],
        out_shape=[
            VM(s, d) if p == PINNED else jax.ShapeDtypeStruct(s, d) for s, d, p in outs
        ],
        compiler_params=pltpu.CompilerParams(vmem_limit_bytes=LIMIT),
        **kw,
    )(*[pltpu.with_memory_space_constraint(a, VM) if p == PINNED else a for a, p in args])


def norm_rows(wide):
    mean = jnp.mean(wide * wide, axis=1, keepdims=True)
    return wide * lax.rsqrt(mean + 1e-06)


def normalize(emb_ref, wide_ref, xh_ref, raw_ref, sems):
    n_parts, size = raw_ref.shape[:2]

    def fetch(i):
        return pltpu.make_async_copy(
            emb_ref.at[pl.ds(i * size, size)], raw_ref.at[i], sems.at[i]
        )

    for i in range(n_parts):
        fetch(i).start()
    for i in range(n_parts):
        rows = slice(i * size, (i + 1) * size)
        fetch(i).wait()
        xh = norm_rows(raw_ref[i].astype(F32)).astype(BF16)
        xh_ref[rows, :] = xh
        wide_ref[rows, :] = xh.astype(F32)


def lane_total(block):
    return jnp.sum(block.T, axis=0, keepdims=True)


def lane_totals(acc_ref, out_ref):
    for t in range(acc_ref.shape[0] // 128):
        block = slice(t * 128, (t + 1) * 128)
        out_ref[:, block] = lane_total(acc_ref[block, :])


def fold_lanes(block):
    total = block[:, 0:128]
    for t in range(1, block.shape[1] // 128):
        total = total + block[:, t * 128 : (t + 1) * 128]
    return total


def fold_rows(block):
    return jnp.sum(block.reshape(block.shape[0] // 8, 8, block.shape[1]), axis=0)


def scores_exp(ch, xh):
    width = xh.shape[1]
    scores = lax.dot_general(ch, xh, (((1,), (1,)), ((), ())), preferred_element_type=F32)
    return jnp.exp(scores * (1.0 / (TAU * width)))


def energy_own(cents_ref, xh_ref, et_ref, ch_ref, acc_ref, r_ref, raw_ref, sems):
    core = place()[2]
    n_blocks = ch_ref.shape[0] // BLK
    parts = BLK // 128

    def fetch(i):
        return pltpu.make_async_copy(
            cents_ref.at[pl.ds(i * parts, parts), core], raw_ref.at[i], sems.at[i]
        )

    for i in range(n_blocks):
        fetch(i).start()
    for i in range(n_blocks):
        fetch(i).wait()
        raw = raw_ref[i].astype(F32).reshape(BLK, ch_ref.shape[1])
        ch_ref[i * BLK : (i + 1) * BLK, :] = norm_rows(raw).astype(BF16)
    r_acc = jnp.zeros((8, xh_ref.shape[0]), F32)
    for i in range(n_blocks):
        rows = slice(i * BLK, (i + 1) * BLK)
        e = scores_exp(ch_ref[rows, :], xh_ref[...])
        et_ref[rows, :] = e
        acc_ref[rows, :] = fold_lanes(e)
        r_acc = r_acc + fold_rows(e)
    r_ref[...] = jnp.sum(r_acc, axis=0, keepdims=True)


def energy_peer(ch_ref, wide_ref, acc_ref, r_own_ref, et_ref, xh_ref, r_ref, s_ref, c_ref, tot_ref):
    n_blocks = ch_ref.shape[0] // BLK
    half = xh_ref.shape[0]
    xh_ref[...] = wide_ref[...].astype(BF16)
    r_acc = jnp.zeros((8, half), F32)
    for i in range(n_blocks):
        rows = slice(i * BLK, (i + 1) * BLK)
        e = scores_exp(ch_ref[rows, :], xh_ref[...])
        et_ref[rows, :] = e
        tot_ref[rows, :] = acc_ref[rows, :] + fold_lanes(e)
        r_acc = r_acc + fold_rows(e)
    r_peer = jnp.sum(r_acc, axis=0, keepdims=True)
    r_ref[:, 0:half] = r_own_ref[...]
    r_ref[:, half:] = r_peer
    s_ref[:, 0:half] = r_peer
    s_ref[:, half:] = r_own_ref[...]
    lane_totals(tot_ref, c_ref)


def total_of(refs, block):
    total = refs[0][:, block]
    for ref in refs[1:]:
        total = total + ref[:, block]
    return total


def spread_block(row):
    return jnp.broadcast_to(row, (128, 128)).T


def column_pass(n_parts, eta_ref, etb_ref, first_c_ref, *refs):
    uo_ref, co_ref, acc_ref = refs[n_parts:]
    n = eta_ref.shape[0]
    u = jnp.sqrt(1.0 / total_of(refs[:n_parts], slice(None)))
    uo_ref[...] = u
    co_ref[:, 0:n] = first_c_ref[...]
    tiles = eta_ref.shape[1] // 128
    ub = [jnp.broadcast_to(u[:, t * 128 : (t + 1) * 128], (8, 128)) for t in range(2 * tiles)]

    def step(i, carry):
        rows = pl.ds(pl.multiple_of(i * 8, 8), 8)
        parts = []
        for t in range(2 * tiles):
            ref = eta_ref if t < tiles else etb_ref
            parts.append(ref[rows, (t % tiles) * 128 : (t % tiles + 1) * 128] * ub[t])
        while len(parts) > 1:
            parts = [a + b for a, b in zip(parts[::2], parts[1::2])]
        acc_ref[rows, :] = parts[0]
        return carry

    lax.fori_loop(0, n // 8, step, 0, unroll=8)
    for t in range(n // 128):
        block = slice(t * 128, (t + 1) * 128)
        co_ref[:, n + t * 128 : n + (t + 1) * 128] = lane_total(acc_ref[block, :])


def row_pass(n_parts, ratio, eta_ref, etb_ref, *refs):
    vo_ref, ro_ref, so_ref, one_ref, two_ref = refs[n_parts:]
    n = eta_ref.shape[0]
    v1 = jnp.sqrt(ratio / total_of(refs[:n_parts], slice(0, n)))
    v2 = jnp.sqrt(v1 * ratio / total_of(refs[:n_parts], slice(n, 2 * n)))
    vo_ref[...] = v2
    for t in range(n // 128):
        block = slice(t * 128, (t + 1) * 128)
        one_ref[block, :] = spread_block(v1[:, block])
        two_ref[block, :] = spread_block(v2[:, block])
    tiles = eta_ref.shape[1] // 128
    zero = jnp.zeros((8, 128), F32)
    for h, ref in ((0, eta_ref), (1, etb_ref)):

        def step(i, carry):
            rows = pl.ds(pl.multiple_of(i * 8, 8), 8)
            b1, b2 = one_ref[rows, :], two_ref[rows, :]
            out1, out2 = [], []
            for t in range(tiles):
                e = ref[rows, t * 128 : (t + 1) * 128]
                out1.append(carry[t] + e * b1)
                out2.append(carry[tiles + t] + e * b2)
            return (*out1, *out2)

        acc = lax.fori_loop(0, n // 8, step, (zero,) * (2 * tiles), unroll=8)
        for t in range(2 * tiles):
            total = jnp.sum(acc[t], axis=0, keepdims=True)
            at = (t // tiles * 2 + h) * tiles + t % tiles
            swapped = (t // tiles * 2 + 1 - h) * tiles + t % tiles
            ro_ref[:, at * 128 : (at + 1) * 128] = total
            so_ref[:, swapped * 128 : (swapped + 1) * 128] = total


def weigh(d, upper, out_ref, eta_ref, etb_ref, xa_ref, xb_ref, ku_ref, u2_ref):
    (at, stride), (_, step) = place()[3:]
    begin = (at ^ d) * stride
    half = eta_ref.shape[1]
    out_ref[256:264, :] = jnp.zeros((8, 512), F32)
    parts = ([], [])
    for k in range(4):
        start = (begin + k * step) * 128 + 64 * upper
        rows = pl.ds(pl.multiple_of(start, 64), 64)
        total = jnp.zeros((64, 128), F32)
        second = jnp.zeros((64, 128), F32)
        for peer, ref in ((False, eta_ref), (True, etb_ref)):
            tiles = []
            for t in range(half // 128):
                lanes = slice(t * 128, (t + 1) * 128)
                at_u = slice(half * peer + t * 128, half * peer + (t + 1) * 128)
                e = ref[rows, lanes]
                scaled = ku_ref[:, at_u] * e
                total = total + scaled
                second = second + u2_ref[:, at_u] * e
                tiles.append(scaled.astype(BF16))
            parts[peer].append(jnp.concatenate(tiles, axis=1))
        lanes = slice(k * 128 + 64 * upper, k * 128 + 64 * upper + 64)
        out_ref[256:257, lanes] = lane_total(total)
        out_ref[257:258, lanes] = lane_total(second)
    out_ref[0:256, :] = jnp.dot(
        jnp.concatenate(parts[0], axis=0), xa_ref[...], preferred_element_type=F32
    ) + jnp.dot(jnp.concatenate(parts[1], axis=0), xb_ref[...], preferred_element_type=F32)


def plan_first(n_parts, big, eta, etb, xa, xb, u_ref, *refs):
    ku_ref, u2_ref, low_ref = refs[n_parts:]
    both = u_ref.shape[1]
    u2 = jnp.sqrt(u_ref[...] / total_of(refs[:n_parts], slice(0, both)))
    u2_ref[...] = u2
    ku_ref[...] = big * jnp.sqrt(u2 / total_of(refs[:n_parts], slice(both, 2 * both)))
    weigh(2, 0, low_ref, eta, etb, xa, xb, ku_ref, u2_ref)


def plan_more(which, *refs):
    for (d, upper), out_ref in zip(which, refs[7:]):
        weigh(d, upper, out_ref, *refs[:6])


def plan_on(d, upper, *refs):
    weigh(d, upper, refs[-1], *refs[:6])
    refs[-1][...] += refs[7][...]


def second_pieces(low0, low1, low3, high0, high1, high3, *outs):
    at = place()[4][0]
    for d in range(4):
        k = at ^ d
        rows = pl.ds(pl.multiple_of(k * 64, 64), 64)
        lanes = pl.ds(pl.multiple_of(k * 128, 128), 128)
        outs[d][0:64, :] = low0[rows, :] + low1[rows, :] + low3[rows, :]
        outs[d][64:128, :] = high0[rows, :] + high1[rows, :] + high3[rows, :]
        low = low0[256:264, lanes] + low1[256:264, lanes] + low3[256:264, lanes]
        high = high0[256:264, lanes] + high1[256:264, lanes] + high3[256:264, lanes]
        outs[d][128:136, 0:128] = low + high
        outs[d][128:136, 128:] = jnp.zeros((8, 384), F32)


def finish(ratio, scale, v_ref, a, b, c, d, new_ref, mass_ref):
    x, z = place()[:2]
    w = (a[...] + b[...]) + (c[...] + d[...])
    v = v_ref[:, pl.ds(pl.multiple_of((x * NZ + z) * 128, 128), 128)]
    v = jnp.sqrt(v * ratio / w[129:130, 0:128])
    mass_ref[...] = v * (w[128:129, 0:128] * scale)
    spread = spread_block(v)
    new_ref[...] = norm_rows(w[0:128, :] * jnp.concatenate([spread] * 4, axis=1))


def local(embeddings, centroids):
    rows, width = embeddings.shape
    all_cents = centroids.shape[0]
    n = all_cents // NC
    both = 2 * rows
    total_rows = float(rows * lax.axis_size("dp"))
    total_cents = float(all_cents * lax.axis_size("cent"))
    ratio = total_rows / total_cents
    tile = 2 * n * rows * width

    wide, xa = call(
        normalize,
        [((rows, width), F32, HERE), ((rows, width), BF16, HERE)],
        (hbm(embeddings), HBM),
        scratch_shapes=[VM((8, rows // 8, width), BF16), pltpu.SemaphoreType.DMA((8,))],
    )
    wide_peer = other_core(wide)
    eta, ch, acc, r_own = call(
        energy_own,
        [
            ((n, rows), F32, PINNED),
            ((n, width), BF16, HERE),
            ((n, 128), F32, HERE),
            ((1, rows), F32, HERE),
        ],
        (hbm(centroids.reshape(n // 128, NC, 128, width)), HBM),
        (xa, HERE),
        scratch_shapes=[
            VM((n // BLK, BLK // 128, 128, width), BF16),
            pltpu.SemaphoreType.DMA((n // BLK,)),
        ],
        cost=2 * tile,
    )
    vec_u = ((1, both), F32, HERE)
    vec_v = ((1, n), F32, HERE)
    etb, xb, r, swapped, c = call(
        energy_peer,
        [((n, rows), F32, PINNED), ((rows, width), BF16, HERE), vec_u, vec_u, vec_v],
        (ch, HERE),
        (wide_peer, HERE),
        (acc, HERE),
        (r_own, HERE),
        scratch_shapes=[VM((n, 128), F32)],
        cost=2 * tile,
    )
    tiles_of_e = ((eta, PINNED), (etb, PINNED))

    def over_rows(c):
        x = [flip_x(c, d) for d in (1, 3, 2)]
        c = (c + x[0]) + (x[1] + x[2])
        return [c, *[flip_z(c, d) for d in (1, 3, 2)]]

    def over_centroids(r, swapped):
        r = r + other_core(swapped)
        return [r, *[flip_y(r, d) for d in (1, 3, 2)]]

    parts = over_centroids(r, swapped)
    u, c = call(
        functools.partial(column_pass, len(parts)),
        [vec_u, ((1, 2 * n), F32, HERE)],
        *tiles_of_e,
        *[(a, HERE) for a in (c, *parts)],
        scratch_shapes=[VM((n, 128), F32)],
        cost=tile // 2,
    )
    parts = over_rows(c)
    v, r, swapped = call(
        functools.partial(row_pass, len(parts), ratio),
        [vec_v, ((1, 2 * both), F32, HERE), ((1, 2 * both), F32, HERE)],
        *tiles_of_e,
        *[(a, HERE) for a in parts],
        scratch_shapes=[VM((n, 128), F32)] * 2,
        cost=tile,
    )
    parts = over_centroids(r, swapped)
    piece = ((264, width), F32, HERE)
    ku, u2, low2 = call(
        functools.partial(plan_first, len(parts), total_cents),
        [vec_u, vec_u, piece],
        *tiles_of_e,
        *[(a, HERE) for a in (xa, xb, u, *parts)],
        cost=tile // 2,
    )
    from_a = first_axis(low2, 1)
    base = (*tiles_of_e, *[(a, HERE) for a in (xa, xb, ku, u2)])

    def plan(which, after):
        return call(
            functools.partial(plan_more, which),
            [piece] * len(which),
            *base,
            (after, LATER),
            cost=tile * len(which) // 2,
        )

    def plan_sum(d, upper, got, after):
        return call(
            functools.partial(plan_on, d, upper),
            [piece],
            *base,
            (after, LATER),
            (got, HERE),
            cost=tile // 2,
        )[0]

    (high2,) = plan(((2, 1),), low2)
    from_b = first_axis(high2, 3)
    (low1,) = plan(((1, 0),), high2)
    low_a = first_axis(low1, 1)
    (high3,) = plan(((3, 1),), low1)
    high_b = first_axis(high3, 3)
    low0, high0 = plan(((0, 0), (0, 1)), high3)
    low3 = plan_sum(3, 0, from_a, low0)
    low_b = first_axis(low3, 3)
    high1 = plan_sum(1, 1, from_b, low3)
    high_a = first_axis(high1, 1)
    pieces = call(
        second_pieces,
        [((136, width), F32, HERE)] * 4,
        *[(a, HERE) for a in (low0, low_a, low_b, high0, high_a, high_b)],
    )
    got = [second_axis(pieces[d], d) for d in (1, 3, 2)]
    scale = (1.0 / total_cents) * (total_cents / total_rows)
    new, mass = call(
        functools.partial(finish, ratio, scale),
        [((128, width), F32, HERE), ((1, 128), F32, HERE)],
        *[(a, HERE) for a in (v, pieces[0], *got)],
    )
    return new, mass.reshape(128)


def solution(mesh):
    in_specs = (P("dp", None), P("cent", None))
    out_specs = (P(("cent", "dp"), None), P(("cent", "dp")))
    return jax.shard_map(local, mesh=mesh, in_specs=in_specs, out_specs=out_specs, check_vma=False)
```

```python
import functools

import jax
import jax.numpy as jnp
from jax import lax
from jax.experimental import pallas as pl
from jax.experimental.pallas import tpu as pltpu
from jax.sharding import PartitionSpec as P

TAU = 0.02
NX, NZ, NC, NY = 4, 4, 2, 4
F32, BF16 = jnp.float32, jnp.bfloat16
VM = pltpu.VMEM
LIMIT = 16 * 1024 * 1024
BLK = 256


def index(x, z, c):
    return (x * NZ + z) * NC + c


def permute(value, target):
    pairs = [
        (index(x, z, c), index(*target(x, z, c)))
        for x in range(NX)
        for z in range(NZ)
        for c in range(NC)
    ]
    return lax.ppermute(value, "dp", pairs)


def other_core(value):
    return permute(value, lambda x, z, c: (x, z, 1 - c))


def first_axis(value, d):
    return permute(value, lambda x, z, c: (x ^ d, z, c) if c == 0 else (x, z ^ d, c))


def second_axis(value, d):
    return permute(value, lambda x, z, c: (x, z ^ d, c) if c == 0 else (x ^ d, z, c))


def cross_plane(value, dx, dz):
    return permute(value, lambda x, z, c: (x ^ dx, z ^ dz, 1 - c))


def cross_y(value, d):
    pairs = [
        (index(x, z, c) * NY + y, index(x, z, 1 - c) * NY + (y ^ d))
        for x in range(NX)
        for z in range(NZ)
        for c in range(NC)
        for y in range(NY)
    ]
    return lax.ppermute(value, ("dp", "cent"), pairs)


def place():
    dp = lax.axis_index("dp")
    core = lax.rem(dp, NC)
    z = lax.rem(lax.div(dp, NC), NZ)
    x = lax.div(dp, NC * NZ)
    flip = core == 1
    first = (jnp.where(flip, z, x), jnp.where(flip, 1, NZ))
    second = (jnp.where(flip, x, z), jnp.where(flip, NZ, 1))
    return x, z, core, first, second


def hbm(value):
    return pltpu.with_memory_space_constraint(value, pltpu.HBM)


HBM, LATER, HERE, PINNED = "hbm", "later", "vmem", "pinned"


def call(body, outs, *args, cost=None, **kw):
    spaces = {HBM: pltpu.HBM, LATER: pltpu.HBM, HERE: VM, PINNED: VM}
    if cost:
        kw["cost_estimate"] = pl.CostEstimate(flops=cost, bytes_accessed=1 << 20, transcendentals=0)
    return pl.pallas_call(
        body,
        in_specs=[pl.BlockSpec(memory_space=spaces[p]) for _, p in args],
        out_specs=[pl.BlockSpec(memory_space=VM) for _ in outs],
        out_shape=[
            VM(s, d) if p == PINNED else jax.ShapeDtypeStruct(s, d) for s, d, p in outs
        ],
        compiler_params=pltpu.CompilerParams(vmem_limit_bytes=LIMIT),
        **kw,
    )(*[pltpu.with_memory_space_constraint(a, VM) if p == PINNED else a for a, p in args])


def norm_rows(wide):
    mean = jnp.mean(wide * wide, axis=1, keepdims=True)
    return wide * lax.rsqrt(mean + 1e-06)


def normalize(emb_ref, wide_ref, xh_ref, raw_ref, sems):
    n_parts, size = raw_ref.shape[:2]

    def fetch(i):
        return pltpu.make_async_copy(
            emb_ref.at[pl.ds(i * size, size)], raw_ref.at[i], sems.at[i]
        )

    for i in range(n_parts):
        fetch(i).start()
    for i in range(n_parts):
        rows = slice(i * size, (i + 1) * size)
        fetch(i).wait()
        xh = norm_rows(raw_ref[i].astype(F32)).astype(BF16)
        xh_ref[rows, :] = xh
        wide_ref[rows, :] = xh.astype(F32)


def lane_total(block):
    return jnp.sum(block.T, axis=0, keepdims=True)


def lane_totals(acc_ref, out_ref):
    for t in range(acc_ref.shape[0] // 128):
        block = slice(t * 128, (t + 1) * 128)
        out_ref[:, block] = lane_total(acc_ref[block, :])


def fold_lanes(block):
    total = block[:, 0:128]
    for t in range(1, block.shape[1] // 128):
        total = total + block[:, t * 128 : (t + 1) * 128]
    return total


def fold_rows(block):
    return jnp.sum(block.reshape(block.shape[0] // 8, 8, block.shape[1]), axis=0)


def scores_exp(ch, xh):
    width = xh.shape[1]
    scores = lax.dot_general(ch, xh, (((1,), (1,)), ((), ())), preferred_element_type=F32)
    return jnp.exp(scores * (1.0 / (TAU * width)))


def energy_own(cents_ref, xh_ref, et_ref, ch_ref, acc_ref, r_ref, raw_ref, sems):
    core = place()[2]
    n_blocks = ch_ref.shape[0] // BLK
    parts = BLK // 128

    def fetch(i):
        return pltpu.make_async_copy(
            cents_ref.at[pl.ds(i * parts, parts), core], raw_ref.at[i], sems.at[i]
        )

    for i in range(n_blocks):
        fetch(i).start()
    for i in range(n_blocks):
        fetch(i).wait()
        raw = raw_ref[i].astype(F32).reshape(BLK, ch_ref.shape[1])
        ch_ref[i * BLK : (i + 1) * BLK, :] = norm_rows(raw).astype(BF16)
    r_acc = jnp.zeros((8, xh_ref.shape[0]), F32)
    for i in range(n_blocks):
        rows = slice(i * BLK, (i + 1) * BLK)
        e = scores_exp(ch_ref[rows, :], xh_ref[...])
        et_ref[rows, :] = e
        acc_ref[rows, :] = fold_lanes(e)
        r_acc = r_acc + fold_rows(e)
    r_ref[...] = jnp.sum(r_acc, axis=0, keepdims=True)


def energy_peer(ch_ref, wide_ref, acc_ref, r_own_ref, et_ref, xh_ref, r_ref, s_ref, c_ref, tot_ref):
    n_blocks = ch_ref.shape[0] // BLK
    half = xh_ref.shape[0]
    xh_ref[...] = wide_ref[...].astype(BF16)
    r_acc = jnp.zeros((8, half), F32)
    for i in range(n_blocks):
        rows = slice(i * BLK, (i + 1) * BLK)
        e = scores_exp(ch_ref[rows, :], xh_ref[...])
        et_ref[rows, :] = e
        tot_ref[rows, :] = acc_ref[rows, :] + fold_lanes(e)
        r_acc = r_acc + fold_rows(e)
    r_peer = jnp.sum(r_acc, axis=0, keepdims=True)
    r_ref[:, 0:half] = r_own_ref[...]
    r_ref[:, half:] = r_peer
    s_ref[:, 0:half] = r_peer
    s_ref[:, half:] = r_own_ref[...]
    lane_totals(tot_ref, c_ref)


def total_of(refs, block):
    total = refs[0][:, block]
    for ref in refs[1:]:
        total = total + ref[:, block]
    return total


def row_total(refs, begin, size):
    block, half = slice(begin, begin + size), size // 2
    other = total_of(refs[1:], block)
    return refs[0][:, block] + jnp.concatenate([other[:, half:], other[:, :half]], axis=1)


def spread_block(row):
    return jnp.broadcast_to(row, (128, 128)).T


def column_pass(n_parts, eta_ref, etb_ref, first_c_ref, *refs):
    uo_ref, co_ref, acc_ref = refs[n_parts:]
    n = eta_ref.shape[0]
    u = jnp.sqrt(1.0 / row_total(refs[:n_parts], 0, uo_ref.shape[1]))
    uo_ref[...] = u
    co_ref[:, 0:n] = first_c_ref[...]
    tiles = eta_ref.shape[1] // 128
    ub = [jnp.broadcast_to(u[:, t * 128 : (t + 1) * 128], (8, 128)) for t in range(2 * tiles)]

    def step(i, carry):
        rows = pl.ds(pl.multiple_of(i * 8, 8), 8)
        parts = []
        for t in range(2 * tiles):
            ref = eta_ref if t < tiles else etb_ref
            parts.append(ref[rows, (t % tiles) * 128 : (t % tiles + 1) * 128] * ub[t])
        while len(parts) > 1:
            parts = [a + b for a, b in zip(parts[::2], parts[1::2])]
        acc_ref[rows, :] = parts[0]
        return carry

    lax.fori_loop(0, n // 8, step, 0, unroll=16)
    for t in range(n // 128):
        block = slice(t * 128, (t + 1) * 128)
        co_ref[:, n + t * 128 : n + (t + 1) * 128] = lane_total(acc_ref[block, :])


def row_pass(n_parts, ratio, eta_ref, etb_ref, *refs):
    vo_ref, ro_ref, so_ref, one_ref, two_ref = refs[n_parts:]
    n = eta_ref.shape[0]
    v1 = jnp.sqrt(ratio / total_of(refs[:n_parts], slice(0, n)))
    v2 = jnp.sqrt(v1 * ratio / total_of(refs[:n_parts], slice(n, 2 * n)))
    vo_ref[...] = v2
    for t in range(n // 128):
        block = slice(t * 128, (t + 1) * 128)
        one_ref[block, :] = spread_block(v1[:, block])
        two_ref[block, :] = spread_block(v2[:, block])
    tiles = eta_ref.shape[1] // 128
    zero = jnp.zeros((8, 128), F32)
    for h, ref in ((0, eta_ref), (1, etb_ref)):

        def step(i, carry):
            rows = pl.ds(pl.multiple_of(i * 8, 8), 8)
            b1, b2 = one_ref[rows, :], two_ref[rows, :]
            out1, out2 = [], []
            for t in range(tiles):
                e = ref[rows, t * 128 : (t + 1) * 128]
                out1.append(carry[t] + e * b1)
                out2.append(carry[tiles + t] + e * b2)
            return (*out1, *out2)

        acc = lax.fori_loop(0, n // 8, step, (zero,) * (2 * tiles), unroll=8)
        for t in range(2 * tiles):
            total = jnp.sum(acc[t], axis=0, keepdims=True)
            at = (t // tiles * 2 + h) * tiles + t % tiles
            swapped = (t // tiles * 2 + 1 - h) * tiles + t % tiles
            ro_ref[:, at * 128 : (at + 1) * 128] = total
            so_ref[:, swapped * 128 : (swapped + 1) * 128] = total


def weigh(d, upper, out_ref, eta_ref, etb_ref, xa_ref, xb_ref, ku_ref, u2_ref):
    (at, stride), (_, step) = place()[3:]
    begin = (at ^ d) * stride
    half = eta_ref.shape[1]
    out_ref[256:264, :] = jnp.zeros((8, 512), F32)
    parts = ([], [])
    for k in range(4):
        start = (begin + k * step) * 128 + 64 * upper
        rows = pl.ds(pl.multiple_of(start, 64), 64)
        total = jnp.zeros((64, 128), F32)
        second = jnp.zeros((64, 128), F32)
        for peer, ref in ((False, eta_ref), (True, etb_ref)):
            tiles = []
            for t in range(half // 128):
                lanes = slice(t * 128, (t + 1) * 128)
                at_u = slice(half * peer + t * 128, half * peer + (t + 1) * 128)
                e = ref[rows, lanes]
                scaled = ku_ref[:, at_u] * e
                total = total + scaled
                second = second + u2_ref[:, at_u] * e
                tiles.append(scaled.astype(BF16))
            parts[peer].append(jnp.concatenate(tiles, axis=1))
        lanes = slice(k * 128 + 64 * upper, k * 128 + 64 * upper + 64)
        out_ref[256:257, lanes] = lane_total(total)
        out_ref[257:258, lanes] = lane_total(second)
    out_ref[0:256, :] = jnp.dot(
        jnp.concatenate(parts[0], axis=0), xa_ref[...], preferred_element_type=F32
    ) + jnp.dot(jnp.concatenate(parts[1], axis=0), xb_ref[...], preferred_element_type=F32)


def plan_first(n_parts, big, eta, etb, xa, xb, u_ref, *refs):
    ku_ref, u2_ref, low_ref = refs[n_parts:]
    both = u_ref.shape[1]
    u2 = jnp.sqrt(u_ref[...] / row_total(refs[:n_parts], 0, both))
    u2_ref[...] = u2
    ku_ref[...] = big * jnp.sqrt(u2 / row_total(refs[:n_parts], both, both))
    weigh(2, 0, low_ref, eta, etb, xa, xb, ku_ref, u2_ref)


def plan_more(which, *refs):
    for (d, upper), out_ref in zip(which, refs[7:]):
        weigh(d, upper, out_ref, *refs[:6])


def plan_on(d, upper, *refs):
    weigh(d, upper, refs[-1], *refs[:6])
    refs[-1][...] += refs[7][...]


def second_pieces(low0, low1, low3, high0, high1, high3, *outs):
    at = place()[4][0]
    for d in range(4):
        k = at ^ d
        rows = pl.ds(pl.multiple_of(k * 64, 64), 64)
        lanes = pl.ds(pl.multiple_of(k * 128, 128), 128)
        outs[d][0:64, :] = low0[rows, :] + low1[rows, :] + low3[rows, :]
        outs[d][64:128, :] = high0[rows, :] + high1[rows, :] + high3[rows, :]
        low = low0[256:264, lanes] + low1[256:264, lanes] + low3[256:264, lanes]
        high = high0[256:264, lanes] + high1[256:264, lanes] + high3[256:264, lanes]
        outs[d][128:136, 0:128] = low + high
        outs[d][128:136, 128:] = jnp.zeros((8, 384), F32)


def finish(ratio, scale, v_ref, a, b, c, d, new_ref, mass_ref):
    x, z = place()[:2]
    w = (a[...] + b[...]) + (c[...] + d[...])
    v = v_ref[:, pl.ds(pl.multiple_of((x * NZ + z) * 128, 128), 128)]
    v = jnp.sqrt(v * ratio / w[129:130, 0:128])
    mass_ref[...] = v * (w[128:129, 0:128] * scale)
    spread = spread_block(v)
    new_ref[...] = norm_rows(w[0:128, :] * jnp.concatenate([spread] * 4, axis=1))


def local(embeddings, centroids):
    rows, width = embeddings.shape
    all_cents = centroids.shape[0]
    n = all_cents // NC
    both = 2 * rows
    total_rows = float(rows * lax.axis_size("dp"))
    total_cents = float(all_cents * lax.axis_size("cent"))
    ratio = total_rows / total_cents
    tile = 2 * n * rows * width

    wide, xa = call(
        normalize,
        [((rows, width), F32, HERE), ((rows, width), BF16, HERE)],
        (hbm(embeddings), HBM),
        scratch_shapes=[VM((8, rows // 8, width), BF16), pltpu.SemaphoreType.DMA((8,))],
    )
    wide_peer = other_core(wide)
    eta, ch, acc, r_own = call(
        energy_own,
        [
            ((n, rows), F32, PINNED),
            ((n, width), BF16, HERE),
            ((n, 128), F32, HERE),
            ((1, rows), F32, HERE),
        ],
        (hbm(centroids.reshape(n // 128, NC, 128, width)), HBM),
        (xa, HERE),
        scratch_shapes=[
            VM((n // BLK, BLK // 128, 128, width), BF16),
            pltpu.SemaphoreType.DMA((n // BLK,)),
        ],
        cost=2 * tile,
    )
    vec_u = ((1, both), F32, HERE)
    vec_v = ((1, n), F32, HERE)
    etb, xb, r, swapped, c = call(
        energy_peer,
        [((n, rows), F32, PINNED), ((rows, width), BF16, HERE), vec_u, vec_u, vec_v],
        (ch, HERE),
        (wide_peer, HERE),
        (acc, HERE),
        (r_own, HERE),
        scratch_shapes=[VM((n, 128), F32)],
        cost=2 * tile,
    )
    tiles_of_e = ((eta, PINNED), (etb, PINNED))

    def over_rows(c):
        x = [cross_plane(c, d, 0) for d in (1, 3, 2, 0)]
        c = (x[0] + x[1]) + (x[2] + x[3])
        return [cross_plane(c, 0, d) for d in (1, 3, 2, 0)]

    def over_centroids(r, swapped):
        r = r + other_core(swapped)
        return [r, *[cross_y(r, d) for d in (1, 3, 2)]]

    parts = over_centroids(r, swapped)
    u, c = call(
        functools.partial(column_pass, len(parts)),
        [vec_u, ((1, 2 * n), F32, HERE)],
        *tiles_of_e,
        *[(a, HERE) for a in (c, *parts)],
        scratch_shapes=[VM((n, 128), F32)],
        cost=tile // 2,
    )
    parts = over_rows(c)
    v, r, swapped = call(
        functools.partial(row_pass, len(parts), ratio),
        [vec_v, ((1, 2 * both), F32, HERE), ((1, 2 * both), F32, HERE)],
        *tiles_of_e,
        *[(a, HERE) for a in parts],
        scratch_shapes=[VM((n, 128), F32)] * 2,
        cost=tile,
    )
    parts = over_centroids(r, swapped)
    piece = ((264, width), F32, HERE)
    ku, u2, low2 = call(
        functools.partial(plan_first, len(parts), total_cents),
        [vec_u, vec_u, piece],
        *tiles_of_e,
        *[(a, HERE) for a in (xa, xb, u, *parts)],
        cost=tile // 2,
    )
    from_a = first_axis(low2, 1)
    base = (*tiles_of_e, *[(a, HERE) for a in (xa, xb, ku, u2)])

    def plan(which, after):
        return call(
            functools.partial(plan_more, which),
            [piece] * len(which),
            *base,
            (after, LATER),
            cost=tile * len(which) // 2,
        )

    def plan_sum(d, upper, got, after):
        return call(
            functools.partial(plan_on, d, upper),
            [piece],
            *base,
            (after, LATER),
            (got, HERE),
            cost=tile // 2,
        )[0]

    (high2,) = plan(((2, 1),), low2)
    from_b = first_axis(high2, 3)
    (low1,) = plan(((1, 0),), high2)
    low_a = first_axis(low1, 1)
    (high3,) = plan(((3, 1),), low1)
    high_b = first_axis(high3, 3)
    low0, high0 = plan(((0, 0), (0, 1)), high3)
    low3 = plan_sum(3, 0, from_a, low0)
    low_b = first_axis(low3, 3)
    high1 = plan_sum(1, 1, from_b, low3)
    high_a = first_axis(high1, 1)
    pieces = call(
        second_pieces,
        [((136, width), F32, HERE)] * 4,
        *[(a, HERE) for a in (low0, low_a, low_b, high0, high_a, high_b)],
    )
    got = [second_axis(pieces[d], d) for d in (1, 3, 2)]
    scale = (1.0 / total_cents) * (total_cents / total_rows)
    new, mass = call(
        functools.partial(finish, ratio, scale),
        [((128, width), F32, HERE), ((1, 128), F32, HERE)],
        *[(a, HERE) for a in (v, pieces[0], *got)],
    )
    return new, mass.reshape(128)


def solution(mesh):
    in_specs = (P("dp", None), P("cent", None))
    out_specs = (P(("cent", "dp"), None), P(("cent", "dp")))
    return jax.shard_map(local, mesh=mesh, in_specs=in_specs, out_specs=out_specs, check_vma=False)
```

```python
import functools

import jax
import jax.numpy as jnp
from jax import lax
from jax.experimental import pallas as pl
from jax.experimental.pallas import tpu as pltpu
from jax.sharding import PartitionSpec as P

TAU = 0.02
NX, NZ, NC, NY = 4, 4, 2, 4
F32, BF16 = jnp.float32, jnp.bfloat16
VM = pltpu.VMEM
LIMIT = 16 * 1024 * 1024
BLK = 256


def index(x, z, c):
    return (x * NZ + z) * NC + c


def permute(value, target):
    pairs = [
        (index(x, z, c), index(*target(x, z, c)))
        for x in range(NX)
        for z in range(NZ)
        for c in range(NC)
    ]
    return lax.ppermute(value, "dp", pairs)


def other_core(value):
    return permute(value, lambda x, z, c: (x, z, 1 - c))


def first_axis(value, d):
    return permute(value, lambda x, z, c: (x ^ d, z, c) if c == 0 else (x, z ^ d, c))


def second_axis(value, d):
    return permute(value, lambda x, z, c: (x, z ^ d, c) if c == 0 else (x ^ d, z, c))


def cross_plane(value, dx, dz):
    return permute(value, lambda x, z, c: (x ^ dx, z ^ dz, 1 - c))


def cross_y(value, d):
    pairs = [
        (index(x, z, c) * NY + y, index(x, z, 1 - c) * NY + (y ^ d))
        for x in range(NX)
        for z in range(NZ)
        for c in range(NC)
        for y in range(NY)
    ]
    return lax.ppermute(value, ("dp", "cent"), pairs)


def place():
    dp = lax.axis_index("dp")
    core = lax.rem(dp, NC)
    z = lax.rem(lax.div(dp, NC), NZ)
    x = lax.div(dp, NC * NZ)
    flip = core == 1
    first = (jnp.where(flip, z, x), jnp.where(flip, 1, NZ))
    second = (jnp.where(flip, x, z), jnp.where(flip, NZ, 1))
    return x, z, core, first, second


def hbm(value):
    return pltpu.with_memory_space_constraint(value, pltpu.HBM)


HBM, LATER, HERE, PINNED = "hbm", "later", "vmem", "pinned"


def call(body, outs, *args, cost=None, **kw):
    spaces = {HBM: pltpu.HBM, LATER: pltpu.HBM, HERE: VM, PINNED: VM}
    if cost:
        kw["cost_estimate"] = pl.CostEstimate(flops=cost, bytes_accessed=1 << 20, transcendentals=0)
    return pl.pallas_call(
        body,
        in_specs=[pl.BlockSpec(memory_space=spaces[p]) for _, p in args],
        out_specs=[pl.BlockSpec(memory_space=VM) for _ in outs],
        out_shape=[
            VM(s, d) if p == PINNED else jax.ShapeDtypeStruct(s, d) for s, d, p in outs
        ],
        compiler_params=pltpu.CompilerParams(vmem_limit_bytes=LIMIT),
        **kw,
    )(*[pltpu.with_memory_space_constraint(a, VM) if p == PINNED else a for a, p in args])


def norm_rows(wide):
    mean = jnp.mean(wide * wide, axis=1, keepdims=True)
    return wide * lax.rsqrt(mean + 1e-06)


def normalize(emb_ref, wide_ref, xh_ref, raw_ref, sems):
    n_parts, size = raw_ref.shape[:2]

    def fetch(i):
        return pltpu.make_async_copy(
            emb_ref.at[pl.ds(i * size, size)], raw_ref.at[i], sems.at[i]
        )

    for i in range(n_parts):
        fetch(i).start()
    for i in range(n_parts):
        rows = slice(i * size, (i + 1) * size)
        fetch(i).wait()
        xh = norm_rows(raw_ref[i].astype(F32)).astype(BF16)
        xh_ref[rows, :] = xh
        wide_ref[rows, :] = xh.astype(F32)


def lane_total(block):
    return jnp.sum(block.T, axis=0, keepdims=True)


def lane_totals(acc_ref, out_ref):
    for t in range(acc_ref.shape[0] // 128):
        block = slice(t * 128, (t + 1) * 128)
        out_ref[:, block] = lane_total(acc_ref[block, :])


def fold_lanes(block):
    total = block[:, 0:128]
    for t in range(1, block.shape[1] // 128):
        total = total + block[:, t * 128 : (t + 1) * 128]
    return total


def fold_rows(block):
    return jnp.sum(block.reshape(block.shape[0] // 8, 8, block.shape[1]), axis=0)


def scores_exp(ch, xh):
    width = xh.shape[1]
    scores = lax.dot_general(ch, xh, (((1,), (1,)), ((), ())), preferred_element_type=F32)
    return jnp.exp(scores * (1.0 / (TAU * width)))


def energy_own(cents_ref, xh_ref, et_ref, ch_ref, acc_ref, r_ref, raw_ref, sems):
    core = place()[2]
    n_blocks = ch_ref.shape[0] // BLK
    parts = BLK // 128

    def fetch(i):
        return pltpu.make_async_copy(
            cents_ref.at[pl.ds(i * parts, parts), core], raw_ref.at[i], sems.at[i]
        )

    for i in range(n_blocks):
        fetch(i).start()
    for i in range(n_blocks):
        fetch(i).wait()
        raw = raw_ref[i].astype(F32).reshape(BLK, ch_ref.shape[1])
        ch_ref[i * BLK : (i + 1) * BLK, :] = norm_rows(raw).astype(BF16)
    r_acc = jnp.zeros((8, xh_ref.shape[0]), F32)
    for i in range(n_blocks):
        rows = slice(i * BLK, (i + 1) * BLK)
        e = scores_exp(ch_ref[rows, :], xh_ref[...])
        et_ref[rows, :] = e
        acc_ref[rows, :] = fold_lanes(e)
        r_acc = r_acc + fold_rows(e)
    r_ref[...] = jnp.sum(r_acc, axis=0, keepdims=True)


def energy_peer(ch_ref, wide_ref, acc_ref, r_own_ref, et_ref, xh_ref, r_ref, s_ref, c_ref, tot_ref):
    n_blocks = ch_ref.shape[0] // BLK
    half = xh_ref.shape[0]
    xh_ref[...] = wide_ref[...].astype(BF16)
    r_acc = jnp.zeros((8, half), F32)
    for i in range(n_blocks):
        rows = slice(i * BLK, (i + 1) * BLK)
        e = scores_exp(ch_ref[rows, :], xh_ref[...])
        et_ref[rows, :] = e
        tot_ref[rows, :] = acc_ref[rows, :] + fold_lanes(e)
        r_acc = r_acc + fold_rows(e)
    r_peer = jnp.sum(r_acc, axis=0, keepdims=True)
    r_ref[:, 0:half] = r_own_ref[...]
    r_ref[:, half:] = r_peer
    s_ref[:, 0:half] = r_peer
    s_ref[:, half:] = r_own_ref[...]
    lane_totals(tot_ref, c_ref)


def total_of(refs, block):
    total = refs[0][:, block]
    for ref in refs[1:]:
        total = total + ref[:, block]
    return total


def row_total(refs, begin, size):
    block, half = slice(begin, begin + size), size // 2
    other = total_of(refs[1:], block)
    return refs[0][:, block] + jnp.concatenate([other[:, half:], other[:, :half]], axis=1)


def spread_block(row):
    return jnp.broadcast_to(row, (128, 128)).T


def column_pass(n_parts, eta_ref, etb_ref, first_c_ref, *refs):
    uo_ref, co_ref, acc_ref = refs[n_parts:]
    n = eta_ref.shape[0]
    u = jnp.sqrt(1.0 / row_total(refs[:n_parts], 0, uo_ref.shape[1]))
    uo_ref[...] = u
    co_ref[:, 0:n] = first_c_ref[...]
    tiles = eta_ref.shape[1] // 128
    ub = [jnp.broadcast_to(u[:, t * 128 : (t + 1) * 128], (8, 128)) for t in range(2 * tiles)]

    def step(i, carry):
        rows = pl.ds(pl.multiple_of(i * 8, 8), 8)
        parts = []
        for t in range(2 * tiles):
            ref = eta_ref if t < tiles else etb_ref
            parts.append(ref[rows, (t % tiles) * 128 : (t % tiles + 1) * 128] * ub[t])
        while len(parts) > 1:
            parts = [a + b for a, b in zip(parts[::2], parts[1::2])]
        acc_ref[rows, :] = parts[0]
        return carry

    lax.fori_loop(0, n // 8, step, 0, unroll=16)
    for t in range(n // 128):
        block = slice(t * 128, (t + 1) * 128)
        co_ref[:, n + t * 128 : n + (t + 1) * 128] = lane_total(acc_ref[block, :])


def row_pass(n_parts, ratio, eta_ref, etb_ref, *refs):
    vo_ref, ro_ref, so_ref, one_ref, two_ref = refs[n_parts:]
    n = eta_ref.shape[0]
    v1 = jnp.sqrt(ratio / total_of(refs[:n_parts], slice(0, n)))
    v2 = jnp.sqrt(v1 * ratio / total_of(refs[:n_parts], slice(n, 2 * n)))
    vo_ref[...] = v2
    for t in range(n // 128):
        block = slice(t * 128, (t + 1) * 128)
        one_ref[block, :] = spread_block(v1[:, block])
        two_ref[block, :] = spread_block(v2[:, block])
    tiles = eta_ref.shape[1] // 128
    zero = jnp.zeros((8, 128), F32)
    for h, ref in ((0, eta_ref), (1, etb_ref)):

        def step(i, carry):
            rows = pl.ds(pl.multiple_of(i * 8, 8), 8)
            b1, b2 = one_ref[rows, :], two_ref[rows, :]
            out1, out2 = [], []
            for t in range(tiles):
                e = ref[rows, t * 128 : (t + 1) * 128]
                out1.append(carry[t] + e * b1)
                out2.append(carry[tiles + t] + e * b2)
            return (*out1, *out2)

        acc = lax.fori_loop(0, n // 8, step, (zero,) * (2 * tiles), unroll=8)
        for t in range(2 * tiles):
            total = jnp.sum(acc[t], axis=0, keepdims=True)
            at = (t // tiles * 2 + h) * tiles + t % tiles
            swapped = (t // tiles * 2 + 1 - h) * tiles + t % tiles
            ro_ref[:, at * 128 : (at + 1) * 128] = total
            so_ref[:, swapped * 128 : (swapped + 1) * 128] = total


def weigh(d, upper, out_ref, eta_ref, etb_ref, xa_ref, xb_ref, ku_ref, u2_ref):
    (at, stride), (_, step) = place()[3:]
    begin = (at ^ d) * stride
    half = eta_ref.shape[1]
    out_ref[256:264, :] = jnp.zeros((8, 512), F32)
    parts = ([], [])
    for k in range(4):
        start = (begin + k * step) * 128 + 64 * upper
        rows = pl.ds(pl.multiple_of(start, 64), 64)
        total = jnp.zeros((64, 128), F32)
        second = jnp.zeros((64, 128), F32)
        for peer, ref in ((False, eta_ref), (True, etb_ref)):
            tiles = []
            for t in range(half // 128):
                lanes = slice(t * 128, (t + 1) * 128)
                at_u = slice(half * peer + t * 128, half * peer + (t + 1) * 128)
                e = ref[rows, lanes]
                scaled = ku_ref[:, at_u] * e
                total = total + scaled
                second = second + u2_ref[:, at_u] * e
                tiles.append(scaled.astype(BF16))
            parts[peer].append(jnp.concatenate(tiles, axis=1))
        lanes = slice(k * 128 + 64 * upper, k * 128 + 64 * upper + 64)
        out_ref[256:257, lanes] = lane_total(total)
        out_ref[257:258, lanes] = lane_total(second)
    out_ref[0:256, :] = jnp.dot(
        jnp.concatenate(parts[0], axis=0), xa_ref[...], preferred_element_type=F32
    ) + jnp.dot(jnp.concatenate(parts[1], axis=0), xb_ref[...], preferred_element_type=F32)


def plan_first(n_parts, big, eta, etb, xa, xb, u_ref, *refs):
    ku_ref, u2_ref, low_ref = refs[n_parts:]
    both = u_ref.shape[1]
    u2 = jnp.sqrt(u_ref[...] / row_total(refs[:n_parts], 0, both))
    u2_ref[...] = u2
    ku_ref[...] = big * jnp.sqrt(u2 / row_total(refs[:n_parts], both, both))
    weigh(2, 0, low_ref, eta, etb, xa, xb, ku_ref, u2_ref)


def plan_more(which, *refs):
    for (d, upper), out_ref in zip(which, refs[7:]):
        weigh(d, upper, out_ref, *refs[:6])


def plan_on(d, upper, *refs):
    weigh(d, upper, refs[-1], *refs[:6])
    refs[-1][...] += refs[7][...]


def second_pieces(low0, low1, low3, high0, high1, high3, *outs):
    at = place()[4][0]
    for d in range(4):
        k = at ^ d
        rows = pl.ds(pl.multiple_of(k * 64, 64), 64)
        lanes = pl.ds(pl.multiple_of(k * 128, 128), 128)
        outs[d][0:64, :] = low0[rows, :] + low1[rows, :] + low3[rows, :]
        outs[d][64:128, :] = high0[rows, :] + high1[rows, :] + high3[rows, :]
        low = low0[256:264, lanes] + low1[256:264, lanes] + low3[256:264, lanes]
        high = high0[256:264, lanes] + high1[256:264, lanes] + high3[256:264, lanes]
        outs[d][128:136, 0:128] = low + high
        outs[d][128:136, 128:] = jnp.zeros((8, 384), F32)


def finish(ratio, scale, v_ref, a, b, c, d, new_ref, mass_ref):
    x, z = place()[:2]
    w = (a[...] + b[...]) + (c[...] + d[...])
    v = v_ref[:, pl.ds(pl.multiple_of((x * NZ + z) * 128, 128), 128)]
    v = jnp.sqrt(v * ratio / w[129:130, 0:128])
    mass_ref[...] = v * (w[128:129, 0:128] * scale)
    spread = spread_block(v)
    new_ref[...] = norm_rows(w[0:128, :] * jnp.concatenate([spread] * 4, axis=1))


def local(embeddings, centroids):
    rows, width = embeddings.shape
    all_cents = centroids.shape[0]
    n = all_cents // NC
    both = 2 * rows
    total_rows = float(rows * lax.axis_size("dp"))
    total_cents = float(all_cents * lax.axis_size("cent"))
    ratio = total_rows / total_cents
    tile = 2 * n * rows * width

    wide, xa = call(
        normalize,
        [((rows, width), F32, HERE), ((rows, width), BF16, HERE)],
        (hbm(embeddings), HBM),
        scratch_shapes=[VM((8, rows // 8, width), BF16), pltpu.SemaphoreType.DMA((8,))],
    )
    wide_peer = other_core(wide)
    eta, ch, acc, r_own = call(
        energy_own,
        [
            ((n, rows), F32, PINNED),
            ((n, width), BF16, HERE),
            ((n, 128), F32, HERE),
            ((1, rows), F32, HERE),
        ],
        (hbm(centroids.reshape(n // 128, NC, 128, width)), HBM),
        (xa, HERE),
        scratch_shapes=[
            VM((n // BLK, BLK // 128, 128, width), BF16),
            pltpu.SemaphoreType.DMA((n // BLK,)),
        ],
        cost=2 * tile,
    )
    vec_u = ((1, both), F32, HERE)
    vec_v = ((1, n), F32, HERE)
    etb, xb, r, swapped, c = call(
        energy_peer,
        [((n, rows), F32, PINNED), ((rows, width), BF16, HERE), vec_u, vec_u, vec_v],
        (ch, HERE),
        (wide_peer, HERE),
        (acc, HERE),
        (r_own, HERE),
        scratch_shapes=[VM((n, 128), F32)],
        cost=2 * tile,
    )
    tiles_of_e = ((eta, PINNED), (etb, PINNED))

    def over_rows(c):
        x = [cross_plane(c, d, 0) for d in (0, 1, 3, 2)]
        c = (x[0] + x[1]) + (x[2] + x[3])
        return [cross_plane(c, 0, d) for d in (0, 1, 3, 2)]

    def over_centroids(r, swapped):
        r = r + other_core(swapped)
        return [r, *[cross_y(r, d) for d in (1, 3, 2)]]

    parts = over_centroids(r, swapped)
    u, c = call(
        functools.partial(column_pass, len(parts)),
        [vec_u, ((1, 2 * n), F32, HERE)],
        *tiles_of_e,
        *[(a, HERE) for a in (c, *parts)],
        scratch_shapes=[VM((n, 128), F32)],
        cost=tile // 2,
    )
    parts = over_rows(c)
    v, r, swapped = call(
        functools.partial(row_pass, len(parts), ratio),
        [vec_v, ((1, 2 * both), F32, HERE), ((1, 2 * both), F32, HERE)],
        *tiles_of_e,
        *[(a, HERE) for a in parts],
        scratch_shapes=[VM((n, 128), F32)] * 2,
        cost=tile,
    )
    parts = over_centroids(r, swapped)
    piece = ((264, width), F32, HERE)
    ku, u2, low2 = call(
        functools.partial(plan_first, len(parts), total_cents),
        [vec_u, vec_u, piece],
        *tiles_of_e,
        *[(a, HERE) for a in (xa, xb, u, *parts)],
        cost=tile // 2,
    )
    from_a = first_axis(low2, 1)
    base = (*tiles_of_e, *[(a, HERE) for a in (xa, xb, ku, u2)])

    def plan(which, after):
        return call(
            functools.partial(plan_more, which),
            [piece] * len(which),
            *base,
            (after, LATER),
            cost=tile * len(which) // 2,
        )

    def plan_sum(d, upper, got, after):
        return call(
            functools.partial(plan_on, d, upper),
            [piece],
            *base,
            (after, LATER),
            (got, HERE),
            cost=tile // 2,
        )[0]

    (high2,) = plan(((2, 1),), low2)
    from_b = first_axis(high2, 3)
    (low1,) = plan(((1, 0),), high2)
    low_a = first_axis(low1, 1)
    (high3,) = plan(((3, 1),), low1)
    high_b = first_axis(high3, 3)
    low0, high0 = plan(((0, 0), (0, 1)), high3)
    low3 = plan_sum(3, 0, from_a, low0)
    low_b = first_axis(low3, 3)
    high1 = plan_sum(1, 1, from_b, low3)
    high_a = first_axis(high1, 1)
    pieces = call(
        second_pieces,
        [((136, width), F32, HERE)] * 4,
        *[(a, HERE) for a in (low0, low_a, low_b, high0, high_a, high_b)],
    )
    got = [second_axis(pieces[d], d) for d in (1, 3, 2)]
    scale = (1.0 / total_cents) * (total_cents / total_rows)
    new, mass = call(
        functools.partial(finish, ratio, scale),
        [((128, width), F32, HERE), ((1, 128), F32, HERE)],
        *[(a, HERE) for a in (v, pieces[0], *got)],
    )
    return new, mass.reshape(128)


def solution(mesh):
    in_specs = (P("dp", None), P("cent", None))
    out_specs = (P(("cent", "dp"), None), P(("cent", "dp")))
    return jax.shard_map(local, mesh=mesh, in_specs=in_specs, out_specs=out_specs, check_vma=False)
```

```python
import functools

import jax
import jax.numpy as jnp
from jax import lax
from jax.experimental import pallas as pl
from jax.experimental.pallas import tpu as pltpu
from jax.sharding import PartitionSpec as P

TAU = 0.02
NX, NZ, NC, NY = 4, 4, 2, 4
F32, BF16 = jnp.float32, jnp.bfloat16
VM = pltpu.VMEM
LIMIT = 16 * 1024 * 1024
BLK = 256


def index(x, z, c):
    return (x * NZ + z) * NC + c


def permute(value, target):
    pairs = [
        (index(x, z, c), index(*target(x, z, c)))
        for x in range(NX)
        for z in range(NZ)
        for c in range(NC)
    ]
    return lax.ppermute(value, "dp", pairs)


def other_core(value):
    return permute(value, lambda x, z, c: (x, z, 1 - c))


def first_axis(value, d):
    return permute(value, lambda x, z, c: (x ^ d, z, c) if c == 0 else (x, z ^ d, c))


def second_axis(value, d):
    return permute(value, lambda x, z, c: (x, z ^ d, c) if c == 0 else (x ^ d, z, c))


def cross_plane(value, dx, dz):
    return permute(value, lambda x, z, c: (x ^ dx, z ^ dz, 1 - c))


def cross_y(value, d):
    pairs = [
        (index(x, z, c) * NY + y, index(x, z, 1 - c) * NY + (y ^ d))
        for x in range(NX)
        for z in range(NZ)
        for c in range(NC)
        for y in range(NY)
    ]
    return lax.ppermute(value, ("dp", "cent"), pairs)


def place():
    dp = lax.axis_index("dp")
    core = lax.rem(dp, NC)
    z = lax.rem(lax.div(dp, NC), NZ)
    x = lax.div(dp, NC * NZ)
    flip = core == 1
    first = (jnp.where(flip, z, x), jnp.where(flip, 1, NZ))
    second = (jnp.where(flip, x, z), jnp.where(flip, NZ, 1))
    return x, z, core, first, second


def hbm(value):
    return pltpu.with_memory_space_constraint(value, pltpu.HBM)


HBM, LATER, HERE, PINNED = "hbm", "later", "vmem", "pinned"


def call(body, outs, *args, cost=None, **kw):
    spaces = {HBM: pltpu.HBM, LATER: pltpu.HBM, HERE: VM, PINNED: VM}
    if cost:
        kw["cost_estimate"] = pl.CostEstimate(flops=cost, bytes_accessed=1 << 20, transcendentals=0)
    return pl.pallas_call(
        body,
        in_specs=[pl.BlockSpec(memory_space=spaces[p]) for _, p in args],
        out_specs=[pl.BlockSpec(memory_space=VM) for _ in outs],
        out_shape=[
            VM(s, d) if p == PINNED else jax.ShapeDtypeStruct(s, d) for s, d, p in outs
        ],
        compiler_params=pltpu.CompilerParams(vmem_limit_bytes=LIMIT),
        **kw,
    )(*[pltpu.with_memory_space_constraint(a, VM) if p == PINNED else a for a, p in args])


def norm_rows(wide):
    mean = jnp.mean(wide * wide, axis=1, keepdims=True)
    return wide * lax.rsqrt(mean + 1e-06)


def normalize(emb_ref, wide_ref, xh_ref, raw_ref, sems):
    n_parts, size = raw_ref.shape[:2]

    def fetch(i):
        return pltpu.make_async_copy(
            emb_ref.at[pl.ds(i * size, size)], raw_ref.at[i], sems.at[i]
        )

    for i in range(n_parts):
        fetch(i).start()
    for i in range(n_parts):
        rows = slice(i * size, (i + 1) * size)
        fetch(i).wait()
        xh = norm_rows(raw_ref[i].astype(F32)).astype(BF16)
        xh_ref[rows, :] = xh
        wide_ref[rows, :] = xh.astype(F32)


def lane_total(block):
    return jnp.sum(block.T, axis=0, keepdims=True)


def lane_totals(acc_ref, out_ref):
    for t in range(acc_ref.shape[0] // 128):
        block = slice(t * 128, (t + 1) * 128)
        out_ref[:, block] = lane_total(acc_ref[block, :])


def fold_lanes(block):
    total = block[:, 0:128]
    for t in range(1, block.shape[1] // 128):
        total = total + block[:, t * 128 : (t + 1) * 128]
    return total


def fold_rows(block):
    return jnp.sum(block.reshape(block.shape[0] // 8, 8, block.shape[1]), axis=0)


def scores_exp(ch, xh):
    width = xh.shape[1]
    scores = lax.dot_general(ch, xh, (((1,), (1,)), ((), ())), preferred_element_type=F32)
    return jnp.exp(scores * (1.0 / (TAU * width)))


def energy_own(cents_ref, xh_ref, et_ref, ch_ref, acc_ref, r_ref, raw_ref, sems):
    core = place()[2]
    n_blocks = ch_ref.shape[0] // BLK
    parts = BLK // 128

    def fetch(i):
        return pltpu.make_async_copy(
            cents_ref.at[pl.ds(i * parts, parts), core], raw_ref.at[i], sems.at[i]
        )

    for i in range(n_blocks):
        fetch(i).start()
    for i in range(n_blocks):
        fetch(i).wait()
        raw = raw_ref[i].astype(F32).reshape(BLK, ch_ref.shape[1])
        ch_ref[i * BLK : (i + 1) * BLK, :] = norm_rows(raw).astype(BF16)
    r_acc = jnp.zeros((8, xh_ref.shape[0]), F32)
    for i in range(n_blocks):
        rows = slice(i * BLK, (i + 1) * BLK)
        e = scores_exp(ch_ref[rows, :], xh_ref[...])
        et_ref[rows, :] = e
        acc_ref[rows, :] = fold_lanes(e)
        r_acc = r_acc + fold_rows(e)
    r_ref[...] = jnp.sum(r_acc, axis=0, keepdims=True)


def energy_peer(ch_ref, wide_ref, acc_ref, r_own_ref, et_ref, xh_ref, r_ref, s_ref, c_ref, tot_ref):
    n_blocks = ch_ref.shape[0] // BLK
    half = xh_ref.shape[0]
    xh_ref[...] = wide_ref[...].astype(BF16)
    r_acc = jnp.zeros((8, half), F32)
    for i in range(n_blocks):
        rows = slice(i * BLK, (i + 1) * BLK)
        e = scores_exp(ch_ref[rows, :], xh_ref[...])
        et_ref[rows, :] = e
        tot_ref[rows, :] = acc_ref[rows, :] + fold_lanes(e)
        r_acc = r_acc + fold_rows(e)
    r_peer = jnp.sum(r_acc, axis=0, keepdims=True)
    r_ref[:, 0:half] = r_own_ref[...]
    r_ref[:, half:] = r_peer
    s_ref[:, 0:half] = r_peer
    s_ref[:, half:] = r_own_ref[...]
    lane_totals(tot_ref, c_ref)


def total_of(refs, block):
    total = refs[0][:, block]
    for ref in refs[1:]:
        total = total + ref[:, block]
    return total


def row_total(refs, begin, size):
    block, half = slice(begin, begin + size), size // 2
    other = total_of(refs[1:], block)
    return refs[0][:, block] + jnp.concatenate([other[:, half:], other[:, :half]], axis=1)


def spread_block(row):
    return jnp.broadcast_to(row, (128, 128)).T


def column_pass(n_parts, eta_ref, etb_ref, first_c_ref, *refs):
    uo_ref, co_ref, acc_ref = refs[n_parts:]
    n = eta_ref.shape[0]
    u = jnp.sqrt(1.0 / row_total(refs[:n_parts], 0, uo_ref.shape[1]))
    uo_ref[...] = u
    co_ref[:, 0:n] = first_c_ref[...]
    tiles = eta_ref.shape[1] // 128
    ub = [jnp.broadcast_to(u[:, t * 128 : (t + 1) * 128], (8, 128)) for t in range(2 * tiles)]

    def step(i, carry):
        rows = pl.ds(pl.multiple_of(i * 8, 8), 8)
        parts = []
        for t in range(2 * tiles):
            ref = eta_ref if t < tiles else etb_ref
            parts.append(ref[rows, (t % tiles) * 128 : (t % tiles + 1) * 128] * ub[t])
        while len(parts) > 1:
            parts = [a + b for a, b in zip(parts[::2], parts[1::2])]
        acc_ref[rows, :] = parts[0]
        return carry

    lax.fori_loop(0, n // 8, step, 0, unroll=16)
    for t in range(n // 128):
        block = slice(t * 128, (t + 1) * 128)
        co_ref[:, n + t * 128 : n + (t + 1) * 128] = lane_total(acc_ref[block, :])


def row_pass(n_parts, ratio, eta_ref, etb_ref, *refs):
    vo_ref, ro_ref, so_ref, one_ref, two_ref = refs[n_parts:]
    n = eta_ref.shape[0]
    v1 = jnp.sqrt(ratio / total_of(refs[:n_parts], slice(0, n)))
    v2 = jnp.sqrt(v1 * ratio / total_of(refs[:n_parts], slice(n, 2 * n)))
    vo_ref[...] = v2
    for t in range(n // 128):
        block = slice(t * 128, (t + 1) * 128)
        one_ref[block, :] = spread_block(v1[:, block])
        two_ref[block, :] = spread_block(v2[:, block])
    tiles = eta_ref.shape[1] // 128
    zero = jnp.zeros((8, 128), F32)
    for h, ref in ((0, eta_ref), (1, etb_ref)):

        def step(i, carry):
            rows = pl.ds(pl.multiple_of(i * 8, 8), 8)
            b1, b2 = one_ref[rows, :], two_ref[rows, :]
            out1, out2 = [], []
            for t in range(tiles):
                e = ref[rows, t * 128 : (t + 1) * 128]
                out1.append(carry[t] + e * b1)
                out2.append(carry[tiles + t] + e * b2)
            return (*out1, *out2)

        acc = lax.fori_loop(0, n // 8, step, (zero,) * (2 * tiles), unroll=16)
        for t in range(2 * tiles):
            total = jnp.sum(acc[t], axis=0, keepdims=True)
            at = (t // tiles * 2 + h) * tiles + t % tiles
            swapped = (t // tiles * 2 + 1 - h) * tiles + t % tiles
            ro_ref[:, at * 128 : (at + 1) * 128] = total
            so_ref[:, swapped * 128 : (swapped + 1) * 128] = total


def weigh(d, upper, out_ref, eta_ref, etb_ref, xa_ref, xb_ref, ku_ref, u2_ref):
    (at, stride), (_, step) = place()[3:]
    begin = (at ^ d) * stride
    half = eta_ref.shape[1]
    out_ref[256:264, :] = jnp.zeros((8, 512), F32)
    parts = ([], [])
    for k in range(4):
        start = (begin + k * step) * 128 + 64 * upper
        rows = pl.ds(pl.multiple_of(start, 64), 64)
        total = jnp.zeros((64, 128), F32)
        second = jnp.zeros((64, 128), F32)
        for peer, ref in ((False, eta_ref), (True, etb_ref)):
            tiles = []
            for t in range(half // 128):
                lanes = slice(t * 128, (t + 1) * 128)
                at_u = slice(half * peer + t * 128, half * peer + (t + 1) * 128)
                e = ref[rows, lanes]
                scaled = ku_ref[:, at_u] * e
                total = total + scaled
                second = second + u2_ref[:, at_u] * e
                tiles.append(scaled.astype(BF16))
            parts[peer].append(jnp.concatenate(tiles, axis=1))
        lanes = slice(k * 128 + 64 * upper, k * 128 + 64 * upper + 64)
        out_ref[256:257, lanes] = lane_total(total)
        out_ref[257:258, lanes] = lane_total(second)
    out_ref[0:256, :] = jnp.dot(
        jnp.concatenate(parts[0], axis=0), xa_ref[...], preferred_element_type=F32
    ) + jnp.dot(jnp.concatenate(parts[1], axis=0), xb_ref[...], preferred_element_type=F32)


def plan_first(n_parts, big, eta, etb, xa, xb, u_ref, *refs):
    ku_ref, u2_ref, low_ref = refs[n_parts:]
    both = u_ref.shape[1]
    u2 = jnp.sqrt(u_ref[...] / row_total(refs[:n_parts], 0, both))
    u2_ref[...] = u2
    ku_ref[...] = big * jnp.sqrt(u2 / row_total(refs[:n_parts], both, both))
    weigh(2, 0, low_ref, eta, etb, xa, xb, ku_ref, u2_ref)


def plan_more(which, *refs):
    for (d, upper), out_ref in zip(which, refs[7:]):
        weigh(d, upper, out_ref, *refs[:6])


def plan_on(d, upper, *refs):
    weigh(d, upper, refs[-1], *refs[:6])
    refs[-1][...] += refs[7][...]


def second_pieces(low0, low1, low3, high0, high1, high3, *outs):
    at = place()[4][0]
    for d in range(4):
        k = at ^ d
        rows = pl.ds(pl.multiple_of(k * 64, 64), 64)
        lanes = pl.ds(pl.multiple_of(k * 128, 128), 128)
        outs[d][0:64, :] = low0[rows, :] + low1[rows, :] + low3[rows, :]
        outs[d][64:128, :] = high0[rows, :] + high1[rows, :] + high3[rows, :]
        low = low0[256:264, lanes] + low1[256:264, lanes] + low3[256:264, lanes]
        high = high0[256:264, lanes] + high1[256:264, lanes] + high3[256:264, lanes]
        outs[d][128:136, 0:128] = low + high
        outs[d][128:136, 128:] = jnp.zeros((8, 384), F32)


def finish(ratio, scale, v_ref, a, b, c, d, new_ref, mass_ref):
    x, z = place()[:2]
    w = (a[...] + b[...]) + (c[...] + d[...])
    v = v_ref[:, pl.ds(pl.multiple_of((x * NZ + z) * 128, 128), 128)]
    v = jnp.sqrt(v * ratio / w[129:130, 0:128])
    mass_ref[...] = v * (w[128:129, 0:128] * scale)
    spread = spread_block(v)
    new_ref[...] = norm_rows(w[0:128, :] * jnp.concatenate([spread] * 4, axis=1))


def local(embeddings, centroids):
    rows, width = embeddings.shape
    all_cents = centroids.shape[0]
    n = all_cents // NC
    both = 2 * rows
    total_rows = float(rows * lax.axis_size("dp"))
    total_cents = float(all_cents * lax.axis_size("cent"))
    ratio = total_rows / total_cents
    tile = 2 * n * rows * width

    wide, xa = call(
        normalize,
        [((rows, width), F32, HERE), ((rows, width), BF16, HERE)],
        (hbm(embeddings), HBM),
        scratch_shapes=[VM((8, rows // 8, width), BF16), pltpu.SemaphoreType.DMA((8,))],
    )
    wide_peer = other_core(wide)
    eta, ch, acc, r_own = call(
        energy_own,
        [
            ((n, rows), F32, PINNED),
            ((n, width), BF16, HERE),
            ((n, 128), F32, HERE),
            ((1, rows), F32, HERE),
        ],
        (hbm(centroids.reshape(n // 128, NC, 128, width)), HBM),
        (xa, HERE),
        scratch_shapes=[
            VM((n // BLK, BLK // 128, 128, width), BF16),
            pltpu.SemaphoreType.DMA((n // BLK,)),
        ],
        cost=2 * tile,
    )
    vec_u = ((1, both), F32, HERE)
    vec_v = ((1, n), F32, HERE)
    etb, xb, r, swapped, c = call(
        energy_peer,
        [((n, rows), F32, PINNED), ((rows, width), BF16, HERE), vec_u, vec_u, vec_v],
        (ch, HERE),
        (wide_peer, HERE),
        (acc, HERE),
        (r_own, HERE),
        scratch_shapes=[VM((n, 128), F32)],
        cost=2 * tile,
    )
    tiles_of_e = ((eta, PINNED), (etb, PINNED))

    def over_rows(c):
        x = [cross_plane(c, d, 0) for d in (0, 1, 3, 2)]
        c = (x[0] + x[1]) + (x[2] + x[3])
        return [cross_plane(c, 0, d) for d in (0, 1, 3, 2)]

    def over_centroids(r, swapped):
        r = r + other_core(swapped)
        return [r, *[cross_y(r, d) for d in (1, 3, 2)]]

    parts = over_centroids(r, swapped)
    u, c = call(
        functools.partial(column_pass, len(parts)),
        [vec_u, ((1, 2 * n), F32, HERE)],
        *tiles_of_e,
        *[(a, HERE) for a in (c, *parts)],
        scratch_shapes=[VM((n, 128), F32)],
        cost=tile // 2,
    )
    parts = over_rows(c)
    v, r, swapped = call(
        functools.partial(row_pass, len(parts), ratio),
        [vec_v, ((1, 2 * both), F32, HERE), ((1, 2 * both), F32, HERE)],
        *tiles_of_e,
        *[(a, HERE) for a in parts],
        scratch_shapes=[VM((n, 128), F32)] * 2,
        cost=tile,
    )
    parts = over_centroids(r, swapped)
    piece = ((264, width), F32, HERE)
    ku, u2, low2 = call(
        functools.partial(plan_first, len(parts), total_cents),
        [vec_u, vec_u, piece],
        *tiles_of_e,
        *[(a, HERE) for a in (xa, xb, u, *parts)],
        cost=tile // 2,
    )
    from_a = first_axis(low2, 1)
    base = (*tiles_of_e, *[(a, HERE) for a in (xa, xb, ku, u2)])

    def plan(which, after):
        return call(
            functools.partial(plan_more, which),
            [piece] * len(which),
            *base,
            (after, LATER),
            cost=tile * len(which) // 2,
        )

    def plan_sum(d, upper, got, after):
        return call(
            functools.partial(plan_on, d, upper),
            [piece],
            *base,
            (after, LATER),
            (got, HERE),
            cost=tile // 2,
        )[0]

    (high2,) = plan(((2, 1),), low2)
    from_b = first_axis(high2, 3)
    (low1,) = plan(((1, 0),), high2)
    low_a = first_axis(low1, 1)
    (high3,) = plan(((3, 1),), low1)
    high_b = first_axis(high3, 3)
    low0, high0 = plan(((0, 0), (0, 1)), high3)
    low3 = plan_sum(3, 0, from_a, low0)
    low_b = first_axis(low3, 3)
    high1 = plan_sum(1, 1, from_b, low3)
    high_a = first_axis(high1, 1)
    pieces = call(
        second_pieces,
        [((136, width), F32, HERE)] * 4,
        *[(a, HERE) for a in (low0, low_a, low_b, high0, high_a, high_b)],
    )
    got = [second_axis(pieces[d], d) for d in (1, 3, 2)]
    scale = (1.0 / total_cents) * (total_cents / total_rows)
    new, mass = call(
        functools.partial(finish, ratio, scale),
        [((128, width), F32, HERE), ((1, 128), F32, HERE)],
        *[(a, HERE) for a in (v, pieces[0], *got)],
    )
    return new, mass.reshape(128)


def solution(mesh):
    in_specs = (P("dp", None), P("cent", None))
    out_specs = (P(("cent", "dp"), None), P(("cent", "dp")))
    return jax.shard_map(local, mesh=mesh, in_specs=in_specs, out_specs=out_specs, check_vma=False)
```
